256 devices in a mesh: leaf: 64 (over y, z, core), sub: 4 (over x).
Axes of the slice: x: 4, y: 4, z: 8, core: 2. Of those that a mesh axis runs over, the one named last changes fastest.
Arguments:
- vectors: bfloat16 [8, 524288], P(None, ('leaf', 'sub')), may hold values from -6 to 6
- basis: bfloat16 [2048, 64, 256], P(('leaf', 'sub')), may hold values from -0.375 to 0.375
- nearfield_dense_blocks: bfloat16 [2048, 256, 768], P(('leaf', 'sub')), may hold values from -0.21875 to 0.21875
- transfer: bfloat16 [2048, 64, 64], P(('leaf', 'sub')), may hold values from -0.125 to 0.125
- far_tree: int32 [2048, 8], P(('leaf', 'sub')), may hold values from 0 to 63, all different within a row; in each aligned block of 8 rows (0 to 7, 8 to 15, ...) at most 2 rows name the same one
- far_offset: int32 [2048, 8], P(('leaf', 'sub')), may hold values from 0 to 31
- far_coupling: bfloat16 [2048, 8, 64, 64], P(('leaf', 'sub')), may hold values from -0.25 to 0.25
- top_source: int32 [64, 8], P('leaf'), may hold values from 0 to 63
- root_coupling_matrix: bfloat16 [64, 8, 64, 64], P('leaf'), may hold values from -0.25 to 0.25
Outputs:
- product: bfloat16 [8, 524288], P(None, ('leaf', 'sub'))
The draws below stay inside these ranges and needn't reach their ends.
Inputs may be any that keep to these rules, and one draw needn't show every extreme that they name: `far_tree`: the 8 leaves of one device (aligned blocks of rows) name one subtree in at most 2 entries in all, and some subtree in exactly 2; the entries of one row are distinct.
All inputs are finite; a program needn't handle non-finite values.
Results may differ from the reference program's by a relative error of at most 0.0037.
Values may be sent and summed in bfloat16 or wider, within the bound.
A program may use at most 64 MiB of HBM per device.

```python
import math
import jax
import jax.numpy as jnp
import numpy as np
from jax import lax

NVEC = 8
RANK = 64
LEAF_PTS = 256
LEAF_DEV = 8
FX = 8
FT = 8
NTREES = 64
LEAF_SUB = 32
NLEAVES = 2048
NPTS = 524288
CAP = 2


def place_ends(result, key, smallest, largest):
    longest = result.shape.index(max(result.shape))
    spots = []
    for shift in (0, 1):
        where = [jax.random.randint(jax.random.fold_in(key, axis), (), 0, length) for axis, length in enumerate(result.shape)]
        where[longest] = (where[longest] + shift) % result.shape[longest]
        spots.append(tuple(where))
    return result.at[spots[0]].set(smallest).at[spots[1]].set(largest)


def levels(key, extent, split, smallest, top_value):
    gain = 1.0
    for dim, blocks in split:
        steps = jax.random.uniform(jax.random.fold_in(jax.random.fold_in(key, 6), dim), (blocks,), jnp.float32, smallest / len(split), top_value / len(split))
        gain = gain * jnp.repeat(jnp.exp(steps), extent[dim] // blocks).reshape((-1,) + (1,) * (len(extent) - 1 - dim))
    return gain


def assign_block(key, own, number, rows, amount, top, bound, skew):
    sequence = jax.random.permutation(key, amount)
    heavy_load, ordinary = shares(amount, rows * top, bound, skew, True), shares(amount, rows * top, bound, skew, False)
    places = jnp.arange(amount)

    def named(tallies, offset_by):
        used = int((tallies > 0).sum())
        fixed = max(1, used // 4)
        passed = fixed + (places - fixed + offset_by * (used - fixed)) % max(1, amount - fixed)
        return jnp.zeros((amount,), jnp.int32).at[sequence[jnp.where(places < fixed, places, passed)]].set(jnp.asarray(tallies, jnp.int32))

    tallies = jnp.where(number % 4 == 0, named(heavy_load, number // 4), named(ordinary, number - number // 4 - 1))
    mixed = jax.random.permutation(jax.random.fold_in(own, 3), amount)
    giver, taker = mixed[0:amount // 2 * 2:2], mixed[1:amount // 2 * 2:2]
    slack = jnp.minimum(tallies[giver] - 1, bound - tallies[taker]) // 2
    slack = jnp.where((giver == sequence[0]) | (taker == sequence[0]) | (tallies[taker] == 0), 0, jnp.maximum(slack, 0))
    passed = jax.random.randint(jax.random.fold_in(own, 4), (amount // 2,), 0, 1 << 20) % (slack + 1)
    tallies = tallies.at[giver].add(-passed).at[taker].add(passed)
    members = jnp.searchsorted(jnp.cumsum(tallies), jnp.arange(rows * top), side="right").astype(jnp.int32)
    table = members.reshape(top, rows).T
    table = table[jax.random.permutation(jax.random.fold_in(own, 1), rows)]
    offset_by = jax.random.randint(jax.random.fold_in(own, 2), (rows, 1), 0, top)
    return jnp.take_along_axis(table, (jnp.arange(top)[None, :] + offset_by) % top, axis=1)


def shares(number_of, total, bound, slope, full):
    portions = [(1 << 20) // math.isqrt(standing ** slope) + 1 for standing in range(1, number_of + 1)]
    largest = bound if full else min(bound, max(-(-total // number_of), total * portions[0] // sum(portions)))
    least = 1 if total - largest >= number_of - 1 else 0
    given, spare = [largest] + [least] * (number_of - 1), total - largest - least * (number_of - 1)
    while spare > 0:
        candidates = [i for i in range(1, number_of) if given[i] < largest] or [i for i in range(1, number_of) if given[i] < bound]
        pool, budget = sum([portions[i] for i in candidates]), spare
        for i in candidates:
            more = min(bound - given[i], max(1, budget * portions[i] // pool), spare)
            given[i] = given[i] + more
            spare = spare - more
    return np.array(given)


def normal_values(key, shape, width, most, shards=(), kind=jnp.bfloat16):
    result = jax.random.normal(key, shape, jnp.float32) * width
    if len(shards) > 0:
        result = levels(key, shape, shards, -0.22, 0.18) * result
    return jnp.clip(result, min=-most, max=most).astype(kind)


def setup_inputs(seed: int = 0) -> dict:
    seeds = jax.random.split(jax.random.key(seed), 10)
    vectors = normal_values(seeds[0], (NVEC, NPTS), 1.0, 6.0, ((1, 256),))
    basis = normal_values(seeds[1], (NLEAVES, RANK, LEAF_PTS), LEAF_PTS ** -0.5, 0.375, ((0, 256),))
    nearfield_dense_blocks = normal_values(seeds[2], (NLEAVES, LEAF_PTS, 3 * LEAF_PTS), (3 * LEAF_PTS) ** -0.5, 0.21875, ((0, 256),))
    transfer = normal_values(seeds[3], (NLEAVES, RANK, RANK), (RANK * LEAF_SUB) ** -0.5, 0.125, ((0, 256),))
    far_tree_keys = jax.random.split(jax.random.fold_in(seeds[4], 1), NLEAVES // LEAF_DEV)
    far_tree_turns = jax.random.permutation(jax.random.fold_in(seeds[4], 3), NLEAVES // LEAF_DEV)
    far_tree = jax.vmap(lambda own, number: assign_block(jax.random.fold_in(seeds[4], 2), own, number, LEAF_DEV, NTREES, FX, CAP, 2))(far_tree_keys, far_tree_turns).reshape((NLEAVES, FX))
    far_offset = place_ends(jax.random.randint(seeds[5], (NLEAVES, FX), 0, LEAF_SUB), jax.random.fold_in(seeds[5], 1), 0, LEAF_SUB - 1).astype(jnp.int32)
    far_coupling = normal_values(seeds[6], (NLEAVES, FX, RANK, RANK), (RANK * FX) ** -0.5, 0.25, ((0, 256),))
    top_source = place_ends(jax.random.randint(seeds[7], (NTREES, FT), 0, NTREES), jax.random.fold_in(seeds[7], 1), 0, NTREES - 1).astype(jnp.int32)
    root_coupling_matrix = normal_values(seeds[8], (NTREES, FT, RANK, RANK), (RANK * FT) ** -0.5, 0.25, ((0, 64),))
    return dict(vectors=vectors, basis=basis, nearfield_dense_blocks=nearfield_dense_blocks, transfer=transfer, far_tree=far_tree, far_offset=far_offset, far_coupling=far_coupling, top_source=top_source, root_coupling_matrix=root_coupling_matrix)


def reference(vectors, basis, nearfield_dense_blocks, transfer, far_tree, far_offset, far_coupling, top_source, root_coupling_matrix):
    leaf_count = vectors.shape[1] // LEAF_PTS
    leaf_vals = vectors.reshape(NVEC, leaf_count, LEAF_PTS)
    leaf_coef = jnp.einsum('lrp,vlp->lrv', basis.astype(jnp.float32), leaf_vals.astype(jnp.float32)).astype(jnp.bfloat16)
    partial_sum = jnp.einsum('lrs,lrv->lsv', transfer.astype(jnp.float32), leaf_coef.astype(jnp.float32))
    node_coef = partial_sum.reshape(NTREES, LEAF_SUB, RANK, NVEC).sum(1).astype(jnp.bfloat16)
    selected_entry = node_coef[top_source]
    root_local_expansion = jnp.einsum('ynoe,ynez->yoz', root_coupling_matrix.astype(jnp.float32), selected_entry.astype(jnp.float32))
    source_index = (far_tree * LEAF_SUB + far_offset).astype(jnp.int32)
    picked = leaf_coef[source_index]
    far_local = jnp.einsum('lfrs,lfsv->lrv', far_coupling.astype(jnp.float32), picked.astype(jnp.float32))
    owner = (jnp.arange(leaf_count) // LEAF_SUB).astype(jnp.int32)
    root_each = root_local_expansion[owner]
    downward = jnp.einsum('lrs,lsv->lrv', transfer.astype(jnp.float32), root_each, precision=lax.Precision.HIGHEST)
    downward_coefficient = (far_local + downward).astype(jnp.bfloat16)
    far_part = jnp.einsum('lrp,lrv->vlp', basis.astype(jnp.float32), downward_coefficient.astype(jnp.float32))
    padded = jnp.pad(vectors, ((0, 0), (LEAF_PTS, LEAF_PTS)))
    blocks = padded.reshape(NVEC, leaf_count + 2, LEAF_PTS)
    neighbor_span = jnp.concatenate([blocks[:, :-2], blocks[:, 1:-1], blocks[:, 2:]], axis=2)
    nearfield_portion = jnp.einsum('fem,ebm->feb', neighbor_span.astype(jnp.float32), nearfield_dense_blocks.astype(jnp.float32))
    return (nearfield_portion + far_part).reshape(NVEC, leaf_count * LEAF_PTS).astype(jnp.bfloat16)
```

```python
import functools

import jax
import jax.numpy as jnp
from jax import lax
from jax.experimental import pallas as pl
from jax.experimental.pallas import tpu as pltpu
from jax.sharding import PartitionSpec as P

MESH = pl.DeviceIdType.MESH
F32 = jnp.float32
BF16 = jnp.bfloat16
NT = (((1,), (1,)), ((), ()))
TREES = 64
SUBS = 4
LEAVES = 8
LINKS = 8
NVEC = 8
RANK = 64
WIDTH = 256


def dot(a, b):
    return jnp.dot(a, b, preferred_element_type=F32)


def dot_nt(a, b):
    return lax.dot_general(a, b, NT, preferred_element_type=F32)


def iota(shape, dim):
    return lax.broadcasted_iota(jnp.int32, shape, dim)


def drain(ref, sem):
    pltpu.make_async_copy(ref, ref, sem).wait()


def kernel(
    vec_hbm, basis_hbm, near_hbm, trans_hbm, tree_hbm, offset_hbm, far_hbm, top_hbm, root_hbm,
    out_ref,
    x_v, basis_v, near_v, trans_v, tree_v, offset_v, far_v, root_v, tree_s, top_s,
    prev_v, next_v, table_send, table_recv, coef_send, coef_recv, node_send, node_recv,
    reply_send, reply_recv, picked_v, rank_v, pairs_v, down_v, local_v,
    sem_x, sem_basis, sem_near, sem_trans, sem_table, sem_far, sem_root, sem_smem,
    halo_send, halo_recv, table_ssem, table_rsem, coef_ssem, coef_rsem,
    node_ssem, node_rsem, reply_ssem, reply_rsem,
):
    me = lax.axis_index("leaf")
    sub = lax.axis_index("sub")
    flat = me * SUBS + sub
    after = lax.rem(flat + 1, TREES * SUBS)
    before = lax.rem(flat + TREES * SUBS - 1, TREES * SUBS)
    after_id = {"leaf": after // SUBS, "sub": lax.rem(after, SUBS)}
    before_id = {"leaf": before // SUBS, "sub": lax.rem(before, SUBS)}

    barrier = pltpu.get_barrier_semaphore()

    def greet(i, carry):
        pl.semaphore_signal(
            barrier, inc=1, device_id={"leaf": lax.rem(me + i, TREES)}, device_id_type=MESH
        )
        return carry

    for i in range(1, SUBS):
        pl.semaphore_signal(
            barrier, inc=1, device_id={"sub": lax.rem(sub + i, SUBS)}, device_id_type=MESH
        )
    pl.semaphore_signal(barrier, inc=1, device_id=after_id, device_id_type=MESH)
    pl.semaphore_signal(barrier, inc=1, device_id=before_id, device_id_type=MESH)
    lax.fori_loop(1, TREES, greet, 0)

    get_tree = pltpu.make_async_copy(tree_hbm, tree_v, sem_table.at[0])
    get_offset = pltpu.make_async_copy(offset_hbm, offset_v, sem_table.at[1])
    get_x = pltpu.make_async_copy(vec_hbm, x_v, sem_x)
    get_basis = pltpu.make_async_copy(basis_hbm, basis_v, sem_basis)
    get_trans = pltpu.make_async_copy(trans_hbm, trans_v, sem_trans)
    get_tree_s = pltpu.make_async_copy(tree_hbm, tree_s, sem_smem.at[0])
    get_top_s = pltpu.make_async_copy(top_hbm, top_s, sem_smem.at[1])
    get_far = pltpu.make_async_copy(far_hbm, far_v, sem_far)
    get_root = pltpu.make_async_copy(root_hbm, root_v, sem_root)
    get_near = [
        pltpu.make_async_copy(near_hbm.at[l], near_v.at[l], sem_near.at[l]) for l in range(LEAVES)
    ]
    for copy in (get_x, get_basis, get_tree, get_offset, get_trans, get_tree_s, get_top_s):
        copy.start()
    get_far.start()
    get_root.start()
    for copy in get_near:
        copy.start()

    get_tree.wait()
    get_offset.wait()
    tree = tree_v[...].astype(F32).astype(BF16)
    offset = offset_v[...].astype(F32).astype(BF16)
    lane = iota((LINKS, 128), 1)
    column = iota((LINKS, 128), 0)
    spread = lax.rem(lane, LINKS) == column
    low = jnp.where(spread & (lane < 64), 1.0, 0.0).astype(BF16)
    high = jnp.where(spread & (lane >= 64), 1.0, 0.0).astype(BF16)
    rows = dot(tree, low) + dot(offset, high)
    own_row = lax.rem(lane, 64) // LINKS == column
    table_row = jnp.sum(jnp.where(own_row, rows, 0.0), axis=0, keepdims=True)
    table_send[...] = table_row
    table_recv[pl.ds(me, 1)] = table_row[None]

    get_x.wait()
    get_basis.wait()
    coefs = []
    for l in range(LEAVES):
        c = dot_nt(x_v[:, l * WIDTH : (l + 1) * WIDTH], basis_v[l]).astype(BF16)
        coefs.append(c)
        wide = c.astype(F32)
        wide = jnp.concatenate([wide, wide], axis=1)
        coef_send[0:NVEC, l, :] = wide
    get_trans.wait()
    partial = dot(coefs[0], trans_v[0])
    for l in range(1, LEAVES):
        partial = partial + dot(coefs[l], trans_v[l])
    coef_send[NVEC] = jnp.concatenate([partial, partial], axis=1)

    pl.semaphore_wait(barrier, TREES - 1 + SUBS - 1 + 2)

    for i in range(1, SUBS):
        pltpu.make_async_remote_copy(
            src_ref=coef_send, dst_ref=coef_recv.at[sub], send_sem=coef_ssem, recv_sem=coef_rsem,
            device_id={"sub": lax.rem(sub + i, SUBS)}, device_id_type=MESH,
        ).start()
    to_after = pltpu.make_async_remote_copy(
        src_ref=vec_hbm.at[:, pl.ds((LEAVES - 1) * WIDTH, WIDTH)], dst_ref=prev_v,
        send_sem=halo_send.at[0], recv_sem=halo_recv.at[0], device_id=after_id, device_id_type=MESH,
    )
    to_before = pltpu.make_async_remote_copy(
        src_ref=vec_hbm.at[:, pl.ds(0, WIDTH)], dst_ref=next_v,
        send_sem=halo_send.at[1], recv_sem=halo_recv.at[1], device_id=before_id, device_id_type=MESH,
    )

    def ask(i, carry):
        peer = lax.rem(me + i, TREES)
        pltpu.make_async_remote_copy(
            src_ref=table_send, dst_ref=table_recv.at[me], send_sem=table_ssem, recv_sem=table_rsem,
            device_id={"leaf": peer}, device_id_type=MESH,
        ).start()
        return carry

    lax.fori_loop(1, TREES, ask, 0)
    to_after.start()
    to_before.start()
    coef_recv[pl.ds(sub, 1)] = coef_send[...][None]

    entry = iota((64, LINKS), 0)
    link = iota((64, LINKS), 1)
    pick_row = jnp.where(entry // LINKS == link, 1.0, 0.0).astype(BF16)
    by_entry = dot(pick_row, tree)
    tree_col = jnp.sum(
        jnp.where(lax.rem(entry, LINKS) == link, by_entry, 0.0), axis=1, keepdims=True
    )
    same = (tree_col == table_row[:, 0:64]) & (iota((64, 64), 1) < iota((64, 64), 0))
    rank_col = jnp.sum(jnp.where(same, 1.0, 0.0), axis=1, keepdims=True)
    rank_v[...] = jnp.broadcast_to(rank_col, (64, 128))

    get_far.wait()
    for l in range(LEAVES):
        for f in range(0, LINKS, 2):
            pairs_v[l, :, f * RANK : (f + 2) * RANK] = jnp.concatenate(
                [far_v[l, f], far_v[l, f + 1]], axis=1
            )

    drain(coef_recv.at[pl.ds(0, SUBS - 1)], coef_rsem)
    node = coef_recv[0, NVEC]
    for i in range(1, SUBS):
        node = node + coef_recv[i, NVEC]
    node = node.astype(BF16).astype(F32)
    left = iota((NVEC // 2, 128), 1) < 64
    node_row = jnp.where(left, node[0 : NVEC // 2], node[NVEC // 2 :]).astype(BF16)
    node_send[...] = node_row
    node_recv[pl.ds(me, 1)] = node_row[None]

    def spread_node(i, carry):
        peer = lax.rem(me + i, TREES)
        pltpu.make_async_remote_copy(
            src_ref=node_send, dst_ref=node_recv.at[me], send_sem=node_ssem, recv_sem=node_rsem,
            device_id={"leaf": peer}, device_id_type=MESH,
        ).start()
        return carry

    lax.fori_loop(1, TREES, spread_node, 0)

    drain(table_recv.at[pl.ds(0, TREES - 1)], table_rsem)
    table = table_recv[:, 0, :]
    asked = table[:, 0:64] == me.astype(F32)
    earlier = jnp.where(iota((64, 64), 0) < iota((64, 64), 1), 1.0, 0.0).astype(BF16)
    order = dot(jnp.where(asked, 1.0, 0.0).astype(BF16), earlier)
    named = jnp.where(asked, table[:, 64:128] + 1.0, 0.0)
    first = jnp.sum(jnp.where(order == 0.0, named, 0.0), axis=1, keepdims=True)
    second = jnp.sum(jnp.where(order == 1.0, named, 0.0), axis=1, keepdims=True)
    leaf_no = (iota((64, 32), 1) + 1).astype(F32)
    onehot = jnp.concatenate(
        [jnp.where(first == leaf_no, 1.0, 0.0), jnp.where(second == leaf_no, 1.0, 0.0)], axis=0
    ).astype(BF16)
    left = iota((64, 128), 1) < 64
    for v in range(NVEC):
        source = coef_recv[:, v].reshape(SUBS * LEAVES, 128).astype(BF16)
        both = dot(onehot, source)
        picked_v[:, v, :] = jnp.where(left, both[0:64], both[64:128])
    reply_send[...] = picked_v[...].astype(BF16)
    reply_recv[pl.ds(me, 1)] = reply_send[pl.ds(me, 1)]

    def reply(i, carry):
        peer = lax.rem(me + i, TREES)
        pltpu.make_async_remote_copy(
            src_ref=reply_send.at[peer], dst_ref=reply_recv.at[me],
            send_sem=reply_ssem, recv_sem=reply_rsem,
            device_id={"leaf": peer}, device_id_type=MESH,
        ).start()
        return carry

    lax.fori_loop(1, TREES, reply, 0)

    to_after.wait_recv()
    to_before.wait_recv()
    zero = jnp.zeros((NVEC, WIDTH), BF16)
    front = jnp.where(flat == 0, zero, prev_v[...])
    back = jnp.where(flat == TREES * SUBS - 1, zero, next_v[...])
    for l in range(LEAVES):
        get_near[l].wait()
        parts = [
            front if l == 0 else x_v[:, (l - 1) * WIDTH : l * WIDTH],
            x_v[:, l * WIDTH : (l + 1) * WIDTH],
            back if l == LEAVES - 1 else x_v[:, (l + 1) * WIDTH : (l + 2) * WIDTH],
        ]
        local_v[:, l * WIDTH : (l + 1) * WIDTH] = dot_nt(
            jnp.concatenate(parts, axis=1), near_v[l]
        )

    get_root.wait()
    get_top_s.wait()
    drain(node_recv.at[pl.ds(0, TREES - 1)], node_rsem)
    root_local = None
    for f in range(LINKS):
        n = node_recv[top_s[0, f]].astype(F32)
        n = jnp.concatenate([n[:, 0:64], n[:, 64:128]], axis=0).astype(BF16)
        term = dot_nt(n, root_v[0, f])
        root_local = term if root_local is None else root_local + term
    hi = root_local.astype(BF16)
    rest = root_local - hi.astype(F32)
    mid = rest.astype(BF16)
    lo = (rest - mid.astype(F32)).astype(BF16)
    for l in range(LEAVES):
        down_v[l] = (
            dot_nt(hi, trans_v[l]) + dot_nt(mid, trans_v[l]) + dot_nt(lo, trans_v[l])
        )

    get_tree_s.wait()
    drain(reply_recv.at[pl.ds(0, TREES - 1)], reply_rsem)
    left = iota((NVEC, 128), 1) < 64
    for l in range(LEAVES):
        parts = []
        for f in range(0, LINKS, 2):
            halves = []
            for j in range(2):
                e = l * LINKS + f + j
                got = reply_recv[tree_s[l, f + j]].astype(F32)
                there = jnp.broadcast_to(rank_v[e : e + 1, :], (NVEC, 128)) == float(j)
                halves.append(jnp.where(there, got, pltpu.roll(got, 64, 1)))
            parts.append(jnp.where(left, halves[0], halves[1]))
        coef = jnp.concatenate(parts, axis=1).astype(BF16)
        down = (dot_nt(coef, pairs_v[l]) + down_v[l]).astype(BF16)
        out_ref[:, l * WIDTH : (l + 1) * WIDTH] = (
            local_v[:, l * WIDTH : (l + 1) * WIDTH] + dot(down, basis_v[l])
        ).astype(BF16)

    to_after.wait_send()
    to_before.wait_send()
    drain(coef_recv.at[pl.ds(0, SUBS - 1)], coef_ssem)
    drain(table_recv.at[pl.ds(0, TREES - 1)], table_ssem)
    drain(node_recv.at[pl.ds(0, TREES - 1)], node_ssem)
    drain(reply_recv.at[pl.ds(0, TREES - 1)], reply_ssem)


def shards(vectors, basis, near, transfer, tree, offset, far, top, root):
    dma = pltpu.SemaphoreType.DMA
    scratch = [
        pltpu.VMEM((NVEC, LEAVES * WIDTH), BF16),
        pltpu.VMEM((LEAVES, RANK, WIDTH), BF16),
        pltpu.VMEM((LEAVES, WIDTH, 3 * WIDTH), BF16),
        pltpu.VMEM((LEAVES, RANK, RANK), BF16),
        pltpu.VMEM((LEAVES, LINKS), jnp.int32),
        pltpu.VMEM((LEAVES, LINKS), jnp.int32),
        pltpu.VMEM((LEAVES, LINKS, RANK, RANK), BF16),
        pltpu.VMEM((1, LINKS, RANK, RANK), BF16),
        pltpu.SMEM((LEAVES, LINKS), jnp.int32),
        pltpu.SMEM((1, LINKS), jnp.int32),
        pltpu.VMEM((NVEC, WIDTH), BF16),
        pltpu.VMEM((NVEC, WIDTH), BF16),
        pltpu.VMEM((1, 128), F32),
        pltpu.VMEM((TREES, 1, 128), F32),
        pltpu.VMEM((NVEC + 1, LEAVES, 128), F32),
        pltpu.VMEM((SUBS, NVEC + 1, LEAVES, 128), F32),
        pltpu.VMEM((NVEC // 2, 128), BF16),
        pltpu.VMEM((TREES, NVEC // 2, 128), BF16),
        pltpu.VMEM((TREES, NVEC, 128), BF16),
        pltpu.VMEM((TREES, NVEC, 128), BF16),
        pltpu.VMEM((TREES, NVEC, 128), F32),
        pltpu.VMEM((64, 128), F32),
        pltpu.VMEM((LEAVES, RANK, LINKS * RANK), BF16),
        pltpu.VMEM((LEAVES, NVEC, RANK), F32),
        pltpu.VMEM((NVEC, LEAVES * WIDTH), F32),
        dma,
        dma,
        dma((LEAVES,)),
        dma,
        dma((2,)),
        dma,
        dma,
        dma((2,)),
        dma((2,)),
        dma((2,)),
        dma,
        dma,
        dma,
        dma,
        dma,
        dma,
        dma,
        dma,
    ]
    return pl.pallas_call(
        kernel,
        out_shape=jax.ShapeDtypeStruct(vectors.shape, BF16),
        in_specs=[pl.BlockSpec(memory_space=pl.ANY)] * 9,
        out_specs=pl.BlockSpec(memory_space=pltpu.VMEM),
        scratch_shapes=scratch,
        compiler_params=pltpu.CompilerParams(
            collective_id=0, has_side_effects=True, vmem_limit_bytes=32 * 2**20
        ),
        name="product",
    )(vectors, basis, near, transfer, tree, offset, far, top, root)


def solution(mesh):
    placed = (
        P(None, ("leaf", "sub")),
        P(("leaf", "sub"), None, None),
        P(("leaf", "sub"), None, None),
        P(("leaf", "sub"), None, None),
        P(("leaf", "sub"), None),
        P(("leaf", "sub"), None),
        P(("leaf", "sub"), None, None, None),
        P("leaf", None),
        P("leaf", None, None, None),
    )
    return jax.shard_map(
        shards, mesh=mesh, in_specs=placed, out_specs=P(None, ("leaf", "sub")), check_vma=False
    )
```

```python
import functools

import jax
import jax.numpy as jnp
from jax import lax
from jax.experimental import pallas as pl
from jax.experimental.pallas import tpu as pltpu
from jax.sharding import PartitionSpec as P

MESH = pl.DeviceIdType.MESH
F32 = jnp.float32
BF16 = jnp.bfloat16
NT = (((1,), (1,)), ((), ()))
TREES = 64
SUBS = 4
LEAVES = 8
LINKS = 8
NVEC = 8
RANK = 64
WIDTH = 256


def dot(a, b):
    return jnp.dot(a, b, preferred_element_type=F32)


def dot_nt(a, b):
    return lax.dot_general(a, b, NT, preferred_element_type=F32)


def iota(shape, dim):
    return lax.broadcasted_iota(jnp.int32, shape, dim)


def drain(ref, sem):
    pltpu.make_async_copy(ref, ref, sem).wait()


def kernel(
    vec_hbm, basis_hbm, near_hbm, trans_hbm, tree_hbm, offset_hbm, far_hbm, top_hbm, root_hbm,
    out_ref,
    x_v, basis_v, near_v, trans_v, tree_v, offset_v, far_v, root_v, tree_s, top_s,
    prev_v, next_v, table_send, table_recv, coef_send, coef_recv, node_send, node_recv,
    reply_send, reply_recv, picked_v, rank_v, pairs_v, down_v, local_v,
    sem_x, sem_basis, sem_near, sem_trans, sem_table, sem_far, sem_root, sem_smem,
    halo_send, halo_recv, table_ssem, table_rsem, coef_ssem, coef_rsem,
    node_ssem, node_rsem, reply_ssem, reply_rsem,
):
    me = lax.axis_index("leaf")
    sub = lax.axis_index("sub")
    flat = me * SUBS + sub
    after = lax.rem(flat + 1, TREES * SUBS)
    before = lax.rem(flat + TREES * SUBS - 1, TREES * SUBS)
    after_id = {"leaf": after // SUBS, "sub": lax.rem(after, SUBS)}
    before_id = {"leaf": before // SUBS, "sub": lax.rem(before, SUBS)}

    barrier = pltpu.get_barrier_semaphore()

    def greet(i, carry):
        pl.semaphore_signal(
            barrier, inc=1, device_id={"leaf": lax.rem(me + i, TREES)}, device_id_type=MESH
        )
        return carry

    for i in range(1, SUBS):
        pl.semaphore_signal(
            barrier, inc=1, device_id={"sub": lax.rem(sub + i, SUBS)}, device_id_type=MESH
        )
    pl.semaphore_signal(barrier, inc=1, device_id=after_id, device_id_type=MESH)
    pl.semaphore_signal(barrier, inc=1, device_id=before_id, device_id_type=MESH)
    lax.fori_loop(1, TREES, greet, 0)

    get_tree = pltpu.make_async_copy(tree_hbm, tree_v, sem_table.at[0])
    get_offset = pltpu.make_async_copy(offset_hbm, offset_v, sem_table.at[1])
    get_x = pltpu.make_async_copy(vec_hbm, x_v, sem_x)
    get_basis = pltpu.make_async_copy(basis_hbm, basis_v, sem_basis)
    get_trans = pltpu.make_async_copy(trans_hbm, trans_v, sem_trans)
    get_tree_s = pltpu.make_async_copy(tree_hbm, tree_s, sem_smem.at[0])
    get_top_s = pltpu.make_async_copy(top_hbm, top_s, sem_smem.at[1])
    get_far = pltpu.make_async_copy(far_hbm, far_v, sem_far)
    get_root = pltpu.make_async_copy(root_hbm, root_v, sem_root)
    get_near = [
        pltpu.make_async_copy(near_hbm.at[l], near_v.at[l], sem_near.at[l]) for l in range(LEAVES)
    ]
    for copy in (get_x, get_basis, get_tree, get_offset, get_trans, get_tree_s, get_top_s):
        copy.start()
    get_far.start()
    get_root.start()
    for copy in get_near:
        copy.start()

    get_tree.wait()
    get_offset.wait()
    tree = tree_v[...].astype(F32).astype(BF16)
    offset = offset_v[...].astype(F32).astype(BF16)
    lane = iota((LINKS, 128), 1)
    column = iota((LINKS, 128), 0)
    spread = lax.rem(lane, LINKS) == column
    low = jnp.where(spread & (lane < 64), 1.0, 0.0).astype(BF16)
    high = jnp.where(spread & (lane >= 64), 1.0, 0.0).astype(BF16)
    rows = dot(tree, low) + dot(offset, high)
    own_row = lax.rem(lane, 64) // LINKS == column
    table_row = jnp.sum(jnp.where(own_row, rows, 0.0), axis=0, keepdims=True)
    table_send[...] = table_row
    table_recv[pl.ds(me, 1)] = table_row[None]

    get_x.wait()
    get_basis.wait()
    coefs = [
        dot_nt(x_v[:, l * WIDTH : (l + 1) * WIDTH], basis_v[l]).astype(BF16) for l in range(LEAVES)
    ]
    for l in range(LEAVES):
        wide = coefs[l].astype(F32)
        coef_send[0:NVEC, l, :] = jnp.concatenate([wide, wide], axis=1)
    get_trans.wait()
    terms = [dot(coefs[l], trans_v[l]) for l in range(LEAVES)]
    partial = functools.reduce(jnp.add, terms)
    coef_send[NVEC] = jnp.concatenate([partial, partial], axis=1)

    pl.semaphore_wait(barrier, TREES - 1 + SUBS - 1 + 2)

    for i in range(1, SUBS):
        pltpu.make_async_remote_copy(
            src_ref=coef_send, dst_ref=coef_recv.at[sub], send_sem=coef_ssem, recv_sem=coef_rsem,
            device_id={"sub": lax.rem(sub + i, SUBS)}, device_id_type=MESH,
        ).start()
    to_after = pltpu.make_async_remote_copy(
        src_ref=vec_hbm.at[:, pl.ds((LEAVES - 1) * WIDTH, WIDTH)], dst_ref=prev_v,
        send_sem=halo_send.at[0], recv_sem=halo_recv.at[0], device_id=after_id, device_id_type=MESH,
    )
    to_before = pltpu.make_async_remote_copy(
        src_ref=vec_hbm.at[:, pl.ds(0, WIDTH)], dst_ref=next_v,
        send_sem=halo_send.at[1], recv_sem=halo_recv.at[1], device_id=before_id, device_id_type=MESH,
    )

    def ask(i, carry):
        peer = lax.rem(me + i, TREES)
        pltpu.make_async_remote_copy(
            src_ref=table_send, dst_ref=table_recv.at[me], send_sem=table_ssem, recv_sem=table_rsem,
            device_id={"leaf": peer}, device_id_type=MESH,
        ).start()
        return carry

    lax.fori_loop(1, TREES, ask, 0)
    to_after.start()
    to_before.start()
    coef_recv[pl.ds(sub, 1)] = coef_send[...][None]

    entry = iota((64, LINKS), 0)
    link = iota((64, LINKS), 1)
    pick_row = jnp.where(entry // LINKS == link, 1.0, 0.0).astype(BF16)
    by_entry = dot(pick_row, tree)
    tree_col = jnp.sum(
        jnp.where(lax.rem(entry, LINKS) == link, by_entry, 0.0), axis=1, keepdims=True
    )
    same = (tree_col == table_row[:, 0:64]) & (iota((64, 64), 1) < iota((64, 64), 0))
    rank_col = jnp.sum(jnp.where(same, 1.0, 0.0), axis=1, keepdims=True)
    rank_v[...] = jnp.broadcast_to(rank_col, (64, 128))

    get_far.wait()
    for l in range(LEAVES):
        for f in range(0, LINKS, 2):
            pairs_v[l, :, f * RANK : (f + 2) * RANK] = jnp.concatenate(
                [far_v[l, f], far_v[l, f + 1]], axis=1
            )

    drain(coef_recv.at[pl.ds(0, SUBS - 1)], coef_rsem)
    node = coef_recv[0, NVEC]
    for i in range(1, SUBS):
        node = node + coef_recv[i, NVEC]
    node = node.astype(BF16).astype(F32)
    left = iota((NVEC // 2, 128), 1) < 64
    node_row = jnp.where(left, node[0 : NVEC // 2], node[NVEC // 2 :]).astype(BF16)
    node_send[...] = node_row
    node_recv[pl.ds(me, 1)] = node_row[None]

    def spread_node(i, carry):
        peer = lax.rem(me + i, TREES)
        pltpu.make_async_remote_copy(
            src_ref=node_send, dst_ref=node_recv.at[me], send_sem=node_ssem, recv_sem=node_rsem,
            device_id={"leaf": peer}, device_id_type=MESH,
        ).start()
        return carry

    lax.fori_loop(1, TREES, spread_node, 0)

    drain(table_recv.at[pl.ds(0, TREES - 1)], table_rsem)
    table = table_recv[:, 0, :]
    asked = table[:, 0:64] == me.astype(F32)
    earlier = jnp.where(iota((64, 64), 0) < iota((64, 64), 1), 1.0, 0.0).astype(BF16)
    order = dot(jnp.where(asked, 1.0, 0.0).astype(BF16), earlier)
    named = jnp.where(asked, table[:, 64:128] + 1.0, 0.0)
    first = jnp.sum(jnp.where(order == 0.0, named, 0.0), axis=1, keepdims=True)
    second = jnp.sum(jnp.where(order == 1.0, named, 0.0), axis=1, keepdims=True)
    leaf_no = (iota((64, 32), 1) + 1).astype(F32)
    onehot = jnp.concatenate(
        [jnp.where(first == leaf_no, 1.0, 0.0), jnp.where(second == leaf_no, 1.0, 0.0)], axis=0
    ).astype(BF16)
    left = iota((64, 128), 1) < 64
    boths = [
        dot(onehot, coef_recv[:, v].reshape(SUBS * LEAVES, 128).astype(BF16)) for v in range(NVEC)
    ]
    for v in range(NVEC):
        picked_v[:, v, :] = jnp.where(left, boths[v][0:64], boths[v][64:128])
    reply_send[...] = picked_v[...].astype(BF16)
    reply_recv[pl.ds(me, 1)] = reply_send[pl.ds(me, 1)]

    def reply(i, carry):
        peer = lax.rem(me + i, TREES)
        pltpu.make_async_remote_copy(
            src_ref=reply_send.at[peer], dst_ref=reply_recv.at[me],
            send_sem=reply_ssem, recv_sem=reply_rsem,
            device_id={"leaf": peer}, device_id_type=MESH,
        ).start()
        return carry

    lax.fori_loop(1, TREES, reply, 0)

    to_after.wait_recv()
    to_before.wait_recv()
    zero = jnp.zeros((NVEC, WIDTH), BF16)
    front = jnp.where(flat == 0, zero, prev_v[...])
    back = jnp.where(flat == TREES * SUBS - 1, zero, next_v[...])
    for l in range(LEAVES):
        get_near[l].wait()
        parts = [
            front if l == 0 else x_v[:, (l - 1) * WIDTH : l * WIDTH],
            x_v[:, l * WIDTH : (l + 1) * WIDTH],
            back if l == LEAVES - 1 else x_v[:, (l + 1) * WIDTH : (l + 2) * WIDTH],
        ]
        local_v[:, l * WIDTH : (l + 1) * WIDTH] = dot_nt(
            jnp.concatenate(parts, axis=1), near_v[l]
        )

    get_root.wait()
    get_top_s.wait()
    drain(node_recv.at[pl.ds(0, TREES - 1)], node_rsem)
    terms = []
    for f in range(LINKS):
        n = node_recv[top_s[0, f]].astype(F32)
        n = jnp.concatenate([n[:, 0:64], n[:, 64:128]], axis=0).astype(BF16)
        terms.append(dot_nt(n, root_v[0, f]))
    root_local = functools.reduce(jnp.add, terms)
    hi = root_local.astype(BF16)
    rest = root_local - hi.astype(F32)
    mid = rest.astype(BF16)
    lo = (rest - mid.astype(F32)).astype(BF16)
    three = jnp.concatenate([hi, mid, lo], axis=0)
    terms = [dot_nt(three, trans_v[l]) for l in range(LEAVES)]
    for l in range(LEAVES):
        t = terms[l]
        down_v[l] = t[0:NVEC] + t[NVEC : 2 * NVEC] + t[2 * NVEC : 3 * NVEC]

    get_tree_s.wait()
    drain(reply_recv.at[pl.ds(0, TREES - 1)], reply_rsem)
    left = iota((NVEC, 128), 1) < 64
    coefs = []
    for l in range(LEAVES):
        parts = []
        for f in range(0, LINKS, 2):
            halves = []
            for j in range(2):
                e = l * LINKS + f + j
                got = reply_recv[tree_s[l, f + j]].astype(F32)
                there = jnp.broadcast_to(rank_v[e : e + 1, :], (NVEC, 128)) == float(j)
                halves.append(jnp.where(there, got, pltpu.roll(got, 64, 1)))
            parts.append(jnp.where(left, halves[0], halves[1]))
        coefs.append(jnp.concatenate(parts, axis=1).astype(BF16))
    fars = [dot_nt(coefs[l], pairs_v[l]) for l in range(LEAVES)]
    downs = [(fars[l] + down_v[l]).astype(BF16) for l in range(LEAVES)]
    outs = [dot(downs[l], basis_v[l]) for l in range(LEAVES)]
    for l in range(LEAVES):
        here = slice(l * WIDTH, (l + 1) * WIDTH)
        out_ref[:, here] = (local_v[:, here] + outs[l]).astype(BF16)

    to_after.wait_send()
    to_before.wait_send()
    drain(coef_recv.at[pl.ds(0, SUBS - 1)], coef_ssem)
    drain(table_recv.at[pl.ds(0, TREES - 1)], table_ssem)
    drain(node_recv.at[pl.ds(0, TREES - 1)], node_ssem)
    drain(reply_recv.at[pl.ds(0, TREES - 1)], reply_ssem)


def shards(vectors, basis, near, transfer, tree, offset, far, top, root):
    dma = pltpu.SemaphoreType.DMA
    scratch = [
        pltpu.VMEM((NVEC, LEAVES * WIDTH), BF16),
        pltpu.VMEM((LEAVES, RANK, WIDTH), BF16),
        pltpu.VMEM((LEAVES, WIDTH, 3 * WIDTH), BF16),
        pltpu.VMEM((LEAVES, RANK, RANK), BF16),
        pltpu.VMEM((LEAVES, LINKS), jnp.int32),
        pltpu.VMEM((LEAVES, LINKS), jnp.int32),
        pltpu.VMEM((LEAVES, LINKS, RANK, RANK), BF16),
        pltpu.VMEM((1, LINKS, RANK, RANK), BF16),
        pltpu.SMEM((LEAVES, LINKS), jnp.int32),
        pltpu.SMEM((1, LINKS), jnp.int32),
        pltpu.VMEM((NVEC, WIDTH), BF16),
        pltpu.VMEM((NVEC, WIDTH), BF16),
        pltpu.VMEM((1, 128), F32),
        pltpu.VMEM((TREES, 1, 128), F32),
        pltpu.VMEM((NVEC + 1, LEAVES, 128), F32),
        pltpu.VMEM((SUBS, NVEC + 1, LEAVES, 128), F32),
        pltpu.VMEM((NVEC // 2, 128), BF16),
        pltpu.VMEM((TREES, NVEC // 2, 128), BF16),
        pltpu.VMEM((TREES, NVEC, 128), BF16),
        pltpu.VMEM((TREES, NVEC, 128), BF16),
        pltpu.VMEM((TREES, NVEC, 128), F32),
        pltpu.VMEM((64, 128), F32),
        pltpu.VMEM((LEAVES, RANK, LINKS * RANK), BF16),
        pltpu.VMEM((LEAVES, NVEC, RANK), F32),
        pltpu.VMEM((NVEC, LEAVES * WIDTH), F32),
        dma,
        dma,
        dma((LEAVES,)),
        dma,
        dma((2,)),
        dma,
        dma,
        dma((2,)),
        dma((2,)),
        dma((2,)),
        dma,
        dma,
        dma,
        dma,
        dma,
        dma,
        dma,
        dma,
    ]
    return pl.pallas_call(
        kernel,
        out_shape=jax.ShapeDtypeStruct(vectors.shape, BF16),
        in_specs=[pl.BlockSpec(memory_space=pl.ANY)] * 9,
        out_specs=pl.BlockSpec(memory_space=pltpu.VMEM),
        scratch_shapes=scratch,
        compiler_params=pltpu.CompilerParams(
            collective_id=0, has_side_effects=True, vmem_limit_bytes=60 * 2**20
        ),
        name="product",
    )(vectors, basis, near, transfer, tree, offset, far, top, root)


def solution(mesh):
    placed = (
        P(None, ("leaf", "sub")),
        P(("leaf", "sub"), None, None),
        P(("leaf", "sub"), None, None),
        P(("leaf", "sub"), None, None),
        P(("leaf", "sub"), None),
        P(("leaf", "sub"), None),
        P(("leaf", "sub"), None, None, None),
        P("leaf", None),
        P("leaf", None, None, None),
    )
    return jax.shard_map(
        shards, mesh=mesh, in_specs=placed, out_specs=P(None, ("leaf", "sub")), check_vma=False
    )
```

```python
import functools

import jax
import jax.numpy as jnp
from jax import lax
from jax.experimental import pallas as pl
from jax.experimental.pallas import tpu as pltpu
from jax.sharding import PartitionSpec as P

MESH = pl.DeviceIdType.MESH
F32 = jnp.float32
BF16 = jnp.bfloat16
NT = (((1,), (1,)), ((), ()))
TREES = 64
SUBS = 4
LEAVES = 8
LINKS = 8
NVEC = 8
RANK = 64
WIDTH = 256
HOMES = 32


def dot(a, b):
    return jnp.dot(a, b, preferred_element_type=F32)


def dot_nt(a, b):
    return lax.dot_general(a, b, NT, preferred_element_type=F32)


def iota(shape, dim):
    return lax.broadcasted_iota(jnp.int32, shape, dim)


def drain(ref, sem):
    pltpu.make_async_copy(ref, ref, sem).wait()


def mirror(leaf):
    return leaf + 14 - 4 * lax.rem(leaf // 2, 8)


def home_leaf(j):
    return (j // 8) * 16 + lax.rem(j, 8)


def slot_of(tree):
    m = tree & 15
    late = m >> 3
    return (late * HOMES + ((tree >> 4) << 3) + ((m ^ (late * 14)) & 7)) & (2 * HOMES - 1)


def kernel(
    vec_hbm, basis_hbm, near_hbm, trans_hbm, tree_hbm, offset_hbm, far_hbm, top_hbm, root_hbm,
    out_ref,
    x_v, basis_v, near_v, trans_v, tree_v, offset_v, far_v, root_v, top_v, slot_v, top_slot_v, client_v,
    slot_s, top_slot_s, client_s,
    table_send, table_recv, coef_send, coef_recv, part_send, part_recv, wide_v, both_v, plan_v,
    node_send, node_recv, node_mine, node_theirs, halo_v,
    reply_send, reply_recv, picked_v, rank_v, pairs_v, down_v, local_v,
    sem_x, sem_basis, sem_near, sem_trans, sem_table, sem_far, sem_root, sem_smem,
    halo_ssem, halo_rsem, table_ssem, table_rsem, coef_ssem, coef_rsem, part_ssem, part_rsem,
    node_ssem, node_rsem, reply_ssem, reply_rsem, fwd_sem, pick_sem, client_sem,
):
    me = lax.axis_index("leaf")
    sub = lax.axis_index("sub")
    late = lax.rem(me, 16) // 8
    other = mirror(me)
    home = me + late * (other - me)
    j = (home // 16) * 8 + lax.rem(home, 16)

    def step(leaf, s, by):
        flat = lax.rem(leaf * SUBS + s + by + TREES * SUBS, TREES * SUBS)
        return flat // SUBS, lax.rem(flat, SUBS)

    def home_of(leaf):
        late = lax.rem(leaf, 16) // 8
        return leaf + late * (mirror(leaf) - leaf), late

    barrier = pltpu.get_barrier_semaphore()

    def announce(leaf, s):
        pl.semaphore_signal(
            barrier, inc=1, device_id={"leaf": leaf, "sub": s}, device_id_type=MESH
        )

    def send(src, dst, ssem, rsem, leaf, s):
        pltpu.make_async_remote_copy(
            src_ref=src, dst_ref=dst, send_sem=ssem, recv_sem=rsem,
            device_id={"leaf": leaf, "sub": s}, device_id_type=MESH,
        ).start()

    for i in range(1, SUBS):
        announce(me, lax.rem(sub + i, SUBS))

    @pl.when(late == 0)
    def _():
        def greet(i, carry):
            announce(lax.rem(me + i, TREES), sub)
            return carry

        for leaf in (me, other):
            for by in (-1, 1):
                announce(*step(leaf, sub, by))
        lax.fori_loop(1, TREES, greet, 0)
        for i in range(1, SUBS):
            announce(other, lax.rem(sub + i, SUBS))

    @pl.when(late == 1)
    def _():
        def greet(i, carry):
            announce(mirror(home_leaf(lax.rem(j + i, HOMES))), sub)
            return carry

        lax.fori_loop(1, HOMES, greet, 0)

    get_tree = pltpu.make_async_copy(tree_hbm, tree_v, sem_table.at[0])
    get_offset = pltpu.make_async_copy(offset_hbm, offset_v, sem_table.at[1])
    get_top = pltpu.make_async_copy(top_hbm, top_v, sem_table.at[2])
    get_x = pltpu.make_async_copy(vec_hbm, x_v, sem_x)
    get_basis = pltpu.make_async_copy(basis_hbm, basis_v, sem_basis)
    get_trans = pltpu.make_async_copy(trans_hbm, trans_v, sem_trans)
    get_far = pltpu.make_async_copy(far_hbm, far_v, sem_far)
    get_root = pltpu.make_async_copy(root_hbm, root_v, sem_root)
    get_near = [
        pltpu.make_async_copy(near_hbm.at[l], near_v.at[l], sem_near.at[l]) for l in range(LEAVES)
    ]
    for copy in (get_tree, get_offset, get_top, get_x, get_basis, get_trans):
        copy.start()
    get_far.start()
    get_root.start()
    for copy in get_near:
        copy.start()

    get_tree.wait()
    get_offset.wait()
    get_top.wait()
    slot_v[...] = slot_of(tree_v[...])
    top_slot_v[...] = slot_of(top_v[...])
    get_slot = pltpu.make_async_copy(slot_v, slot_s, sem_smem.at[0])
    get_top_slot = pltpu.make_async_copy(top_slot_v, top_slot_s, sem_smem.at[1])
    get_slot.start()
    get_top_slot.start()
    tree = tree_v[...].astype(F32).astype(BF16)
    offset = offset_v[...].astype(F32).astype(BF16)
    lane = iota((LINKS, 128), 1)
    column = iota((LINKS, 128), 0)
    low = jnp.where((lax.rem(lane, LINKS) == column) & (lane < 64), 1.0, 0.0).astype(BF16)
    rows = dot(tree, low) * 32.0 + dot(offset, low)
    own_row = lane // LINKS == column
    table_row = jnp.sum(jnp.where(own_row, rows, 0.0), axis=0, keepdims=True)
    table_row = table_row.astype(jnp.int32)
    table_send[...] = table_row

    get_x.wait()
    get_basis.wait()
    coefs = [
        dot_nt(x_v[:, l * WIDTH : (l + 1) * WIDTH], basis_v[l]).astype(BF16) for l in range(LEAVES)
    ]
    for l in range(0, LEAVES, 2):
        coef_send[l // 2] = jnp.concatenate(
            [coefs[l].astype(F32), coefs[l + 1].astype(F32)], axis=1
        ).astype(BF16)
    get_trans.wait()
    terms = [dot(coefs[l], trans_v[l]) for l in range(LEAVES)]
    partial = functools.reduce(jnp.add, terms)
    part_send[...] = jnp.concatenate([partial[0 : NVEC // 2], partial[NVEC // 2 :]], axis=1)

    def send_coefs(leaf, s):
        send(coef_send, coef_recv.at[late * SUBS + sub], coef_ssem, coef_rsem.at[late], leaf, s)
        send(part_send, part_recv.at[late, sub], part_ssem, part_rsem.at[late], leaf, s)

    @pl.when(late == 0)
    def _():
        pl.semaphore_wait(barrier, HOMES - 1 + SUBS - 1 + 2)
        for i in range(1, SUBS):
            send_coefs(me, lax.rem(sub + i, SUBS))
        coef_recv[pl.ds(sub, 1)] = coef_send[...][None]
        part_recv[0, pl.ds(sub, 1)] = part_send[...][None]

    @pl.when(late == 1)
    def _():
        pl.semaphore_wait(barrier, 2 * HOMES - 1 + 2 * (SUBS - 1) + 2)
        for i in range(SUBS):
            send_coefs(other, lax.rem(sub + i, SUBS))
        for i in range(1, SUBS):
            send(
                coef_send, coef_recv.at[SUBS + sub], coef_ssem, coef_rsem.at[1],
                me, lax.rem(sub + i, SUBS),
            )
        coef_recv[pl.ds(SUBS + sub, 1)] = coef_send[...][None]

    @pl.when(late == 0)
    def _():
        table_recv[pl.ds(j, 1)] = table_send[...][None]

        def ask(i, carry):
            leaf = home_leaf(lax.rem(j + i, HOMES))
            send(table_send, table_recv.at[j], table_ssem, table_rsem.at[0], leaf, sub)
            return carry

        lax.fori_loop(1, HOMES, ask, 0)

    @pl.when(late == 1)
    def _():
        def ask(i, carry):
            leaf = home_leaf(lax.rem(j + i, HOMES))
            send(table_send, table_recv.at[HOMES + j], table_ssem, table_rsem.at[1], leaf, sub)
            return carry

        def ask_late(i, carry):
            leaf = mirror(home_leaf(lax.rem(j + i, HOMES)))
            send(table_send, table_recv.at[HOMES + j], table_ssem, table_rsem.at[1], leaf, sub)
            return carry

        send(top_slot_v, client_v, client_sem.at[0], client_sem.at[1], other, sub)
        lax.fori_loop(0, HOMES, ask, 0)
        lax.fori_loop(1, HOMES, ask_late, 0)
        table_recv[pl.ds(HOMES + j, 1)] = table_send[...][None]

    for side, by, start in ((0, 1, (LEAVES - 1) * WIDTH), (1, -1, 0)):
        leaf, s = step(me, sub, by)
        leaf, kind = home_of(leaf)
        send(
            vec_hbm.at[:, pl.ds(start, WIDTH)], halo_v.at[kind, side],
            halo_ssem, halo_rsem.at[kind, side], leaf, s,
        )

    entry = iota((64, LINKS), 0)
    link = iota((64, LINKS), 1)
    pick_row = jnp.where(entry // LINKS == link, 1.0, 0.0).astype(BF16)
    by_entry = dot(pick_row, tree)
    tree_col = jnp.sum(
        jnp.where(lax.rem(entry, LINKS) == link, by_entry, 0.0), axis=1, keepdims=True
    )
    tree_row = (table_row[:, 0:64] >> 5).astype(F32)
    same = (tree_col == tree_row) & (iota((64, 64), 1) < iota((64, 64), 0))
    rank_col = jnp.sum(jnp.where(same, 1.0, 0.0), axis=1, keepdims=True)
    rank_v[...] = jnp.broadcast_to(rank_col, (64, 128))

    get_far.wait()
    for l in range(LEAVES):
        for f in range(0, LINKS, 2):
            pairs_v[l, :, f * RANK : (f + 2) * RANK] = jnp.concatenate(
                [far_v[l, f], far_v[l, f + 1]], axis=1
            )

    def near(l, before, after):
        middle = x_v[:, l * WIDTH : (l + 1) * WIDTH]
        span = jnp.concatenate([before, middle, after], axis=1)
        local_v[:, l * WIDTH : (l + 1) * WIDTH] = dot_nt(span, near_v[l])

    for l in range(1, LEAVES - 1):
        get_near[l].wait()
        near(l, x_v[:, (l - 1) * WIDTH : l * WIDTH], x_v[:, (l + 1) * WIDTH : (l + 2) * WIDTH])
    get_near[0].wait()
    get_near[LEAVES - 1].wait()
    get_root.wait()
    get_slot.wait()
    get_top_slot.wait()

    earlier = jnp.where(iota((64, 64), 0) < iota((64, 64), 1), 1.0, 0.0).astype(BF16)
    row_no = iota((HOMES, SUBS * LEAVES), 1) + 1

    def plan(kind, asker, tree_id):
        table = table_recv[asker * HOMES : (asker + 1) * HOMES, 0, :][:, 0:64]
        asked = (table >> 5) == tree_id
        pair = (table & 31) >> 1
        odd = table & 1
        order = dot(jnp.where(asked, 1.0, 0.0).astype(BF16), earlier)
        rows = (
            jnp.where(asked & (order == 0.0), (pair + 16 * odd + 1).astype(F32), 0.0),
            jnp.where(asked & (order == 1.0), (pair + 16 - 16 * odd + 1).astype(F32), 0.0),
        )
        plan_v[2 * asker + kind] = jnp.concatenate(
            [
                jnp.where(
                    jnp.sum(r, axis=1, keepdims=True).astype(jnp.int32) == row_no, 1.0, 0.0
                )
                for r in rows
            ],
            axis=0,
        ).astype(BF16)

    def fill(kind, asker):
        at = 2 * asker + kind
        left = iota((HOMES, 128), 1) < 64
        onehot = plan_v[at]
        boths = [dot(onehot, both_v[kind, v]) for v in range(NVEC)]
        for v in range(NVEC):
            picked_v[at, :, v, :] = jnp.where(left, boths[v][0:HOMES], boths[v][HOMES:])
        reply_send[at * HOMES : (at + 1) * HOMES] = picked_v[at].astype(BF16)

    def sums(kind):
        node = functools.reduce(jnp.add, [part_recv[kind, i] for i in range(SUBS)]).astype(BF16)
        node_send[kind] = node
        node_recv[pl.ds(kind * HOMES + j, 1)] = node[None]

    def unpack(kind):
        pairs = coef_recv[kind * SUBS : (kind + 1) * SUBS]
        wide_v[kind] = pairs.reshape(SUBS * LEAVES // 2, NVEC, 128).astype(F32)
        for v in range(NVEC):
            straight = wide_v[kind, :, v, :]
            turned = pltpu.roll(straight, 64, 1)
            both_v[kind, v] = jnp.concatenate([straight, turned], axis=0).astype(BF16)

    def spread_nodes(kind):
        def one(i, carry):
            leaf = home_leaf(lax.rem(j + i, HOMES))
            send(node_send.at[kind], node_recv.at[kind * HOMES + j], node_ssem, node_rsem, leaf, sub)
            return carry

        lax.fori_loop(1, HOMES, one, 0)

    def reply(kind, asker):
        def one(i, carry):
            to = lax.rem(j + i, HOMES)
            leaf = home_leaf(to)
            if asker:
                leaf = mirror(leaf)
            send(
                reply_send.at[(2 * asker + kind) * HOMES + to], reply_recv.at[kind * HOMES + j],
                reply_ssem, reply_rsem, leaf, sub,
            )
            return carry

        lax.fori_loop(0 if kind < asker else 1, HOMES, one, 0)
        if kind >= asker:
            reply_recv[pl.ds(kind * HOMES + j, 1)] = reply_send[
                pl.ds((2 * asker + kind) * HOMES + j, 1)
            ]

    def near_ends():
        zero = jnp.zeros((NVEC, WIDTH), BF16)
        first = (me == 0) & (sub == 0)
        last = (me == TREES - 1) & (sub == SUBS - 1)
        near(0, jnp.where(first, zero, halo_v[0, 0]), x_v[:, WIDTH : 2 * WIDTH])
        near(
            LEAVES - 1,
            x_v[:, (LEAVES - 2) * WIDTH : (LEAVES - 1) * WIDTH],
            jnp.where(last, zero, halo_v[0, 1]),
        )

    @pl.when(late == 0)
    def _():
        drain(part_recv.at[0, pl.ds(0, SUBS - 1)], part_rsem.at[0])
        sums(0)
        spread_nodes(0)
        drain(coef_recv.at[pl.ds(0, SUBS - 1)], coef_rsem.at[0])
        unpack(0)
        drain(table_recv.at[pl.ds(0, HOMES - 1)], table_rsem.at[0])
        plan(0, 0, me)
        fill(0, 0)
        reply(0, 0)
        plan(1, 0, other)
        drain(part_recv.at[1], part_rsem.at[1])
        sums(1)
        spread_nodes(1)
        drain(coef_recv.at[pl.ds(SUBS, SUBS)], coef_rsem.at[1])
        unpack(1)
        fill(1, 0)
        reply(1, 0)
        drain(table_recv.at[pl.ds(0, HOMES)], table_rsem.at[1])
        drain(client_v, client_sem.at[1])
        get_client = pltpu.make_async_copy(client_v, client_s, sem_smem.at[0])
        get_client.start()
        plan(0, 1, me)
        fill(0, 1)
        reply(0, 1)
        for kind in range(2):
            for side in range(2):
                drain(halo_v.at[kind, side], halo_rsem.at[kind, side])
        send(halo_v.at[1], halo_v.at[0], fwd_sem.at[0], fwd_sem.at[1], other, sub)
        near_ends()
        get_client.wait()
        drain(node_recv.at[pl.ds(0, 2 * HOMES - 2)], node_rsem)
        for f in range(LINKS):
            node_theirs[f] = node_recv[client_s[0, f]]
        send(node_theirs, node_mine, pick_sem.at[0], pick_sem.at[1], other, sub)
        for f in range(LINKS):
            node_mine[f] = node_recv[top_slot_s[0, f]]

    @pl.when(late == 1)
    def _():
        drain(coef_recv.at[pl.ds(0, SUBS - 1)], coef_rsem.at[1])
        unpack(1)
        drain(table_recv.at[pl.ds(0, HOMES - 1)], table_rsem.at[1])
        plan(1, 1, me)
        fill(1, 1)
        reply(1, 1)
        drain(halo_v.at[0], fwd_sem.at[1])
        near_ends()
        drain(node_mine, pick_sem.at[1])

    terms = []
    for f in range(LINKS):
        n = node_mine[f].astype(F32)
        n = jnp.concatenate([n[:, 0:64], n[:, 64:128]], axis=0).astype(BF16)
        terms.append(dot_nt(n, root_v[0, f]))
    root_local = functools.reduce(jnp.add, terms)
    hi = root_local.astype(BF16)
    rest = root_local - hi.astype(F32)
    mid = rest.astype(BF16)
    lo = (rest - mid.astype(F32)).astype(BF16)
    three = jnp.concatenate([hi, mid, lo], axis=0)
    terms = [dot_nt(three, trans_v[l]) for l in range(LEAVES)]
    for l in range(LEAVES):
        t = terms[l]
        down_v[l] = t[0:NVEC] + t[NVEC : 2 * NVEC] + t[2 * NVEC : 3 * NVEC]

    @pl.when(late == 0)
    def _():
        drain(reply_recv.at[pl.ds(0, 2 * HOMES - 2)], reply_rsem)

    @pl.when(late == 1)
    def _():
        drain(reply_recv.at[pl.ds(0, 2 * HOMES - 1)], reply_rsem)

    left = iota((NVEC, 128), 1) < 64
    coefs = []
    for l in range(LEAVES):
        parts = []
        for f in range(0, LINKS, 2):
            halves = []
            for k in range(2):
                e = l * LINKS + f + k
                got = reply_recv[slot_s[l, f + k]].astype(F32)
                there = jnp.broadcast_to(rank_v[e : e + 1, :], (NVEC, 128)) == float(k)
                halves.append(jnp.where(there, got, pltpu.roll(got, 64, 1)))
            parts.append(jnp.where(left, halves[0], halves[1]))
        coefs.append(jnp.concatenate(parts, axis=1).astype(BF16))
    fars = [dot_nt(coefs[l], pairs_v[l]) for l in range(LEAVES)]
    downs = [(fars[l] + down_v[l]).astype(BF16) for l in range(LEAVES)]
    outs = [dot(downs[l], basis_v[l]) for l in range(LEAVES)]
    for l in range(LEAVES):
        here = slice(l * WIDTH, (l + 1) * WIDTH)
        out_ref[:, here] = (local_v[:, here] + outs[l]).astype(BF16)

    drain(halo_v.at[0], halo_ssem)

    @pl.when(late == 0)
    def _():
        drain(coef_recv.at[pl.ds(0, SUBS - 1)], coef_ssem)
        drain(part_recv.at[0, pl.ds(0, SUBS - 1)], part_ssem)
        drain(table_recv.at[pl.ds(0, HOMES - 1)], table_ssem)
        drain(node_recv.at[pl.ds(0, 2 * HOMES - 2)], node_ssem)
        drain(reply_send.at[pl.ds(0, 3 * HOMES - 2)], reply_ssem)
        drain(halo_v.at[1], fwd_sem.at[0])
        drain(node_theirs, pick_sem.at[0])

    @pl.when(late == 1)
    def _():
        drain(coef_recv.at[pl.ds(0, 2 * SUBS - 1)], coef_ssem)
        drain(part_recv.at[0], part_ssem)
        drain(table_recv.at[pl.ds(0, 2 * HOMES - 1)], table_ssem)
        drain(client_v, client_sem.at[0])
        drain(reply_send.at[pl.ds(0, HOMES - 1)], reply_ssem)


def shards(vectors, basis, near, transfer, tree, offset, far, top, root):
    dma = pltpu.SemaphoreType.DMA
    i32 = jnp.int32
    scratch = [
        pltpu.VMEM((NVEC, LEAVES * WIDTH), BF16),
        pltpu.VMEM((LEAVES, RANK, WIDTH), BF16),
        pltpu.VMEM((LEAVES, WIDTH, 3 * WIDTH), BF16),
        pltpu.VMEM((LEAVES, RANK, RANK), BF16),
        pltpu.VMEM((LEAVES, LINKS), i32),
        pltpu.VMEM((LEAVES, LINKS), i32),
        pltpu.VMEM((LEAVES, LINKS, RANK, RANK), BF16),
        pltpu.VMEM((1, LINKS, RANK, RANK), BF16),
        pltpu.VMEM((1, LINKS), i32),
        pltpu.VMEM((LEAVES, LINKS), i32),
        pltpu.VMEM((1, LINKS), i32),
        pltpu.VMEM((1, LINKS), i32),
        pltpu.SMEM((LEAVES, LINKS), i32),
        pltpu.SMEM((1, LINKS), i32),
        pltpu.SMEM((1, LINKS), i32),
        pltpu.VMEM((1, 128), i32),
        pltpu.VMEM((2 * HOMES, 1, 128), i32),
        pltpu.VMEM((LEAVES // 2, NVEC, 128), BF16),
        pltpu.VMEM((2 * SUBS, LEAVES // 2, NVEC, 128), BF16),
        pltpu.VMEM((NVEC // 2, 128), F32),
        pltpu.VMEM((2, SUBS, NVEC // 2, 128), F32),
        pltpu.VMEM((2, SUBS * LEAVES // 2, NVEC, 128), F32),
        pltpu.VMEM((2, NVEC, SUBS * LEAVES, 128), BF16),
        pltpu.VMEM((4, 2 * HOMES, SUBS * LEAVES), BF16),
        pltpu.VMEM((2, NVEC // 2, 128), BF16),
        pltpu.VMEM((2 * HOMES, NVEC // 2, 128), BF16),
        pltpu.VMEM((LINKS, NVEC // 2, 128), BF16),
        pltpu.VMEM((LINKS, NVEC // 2, 128), BF16),
        pltpu.VMEM((2, 2, NVEC, WIDTH), BF16),
        pltpu.VMEM((4 * HOMES, NVEC, 128), BF16),
        pltpu.VMEM((2 * HOMES, NVEC, 128), BF16),
        pltpu.VMEM((4, HOMES, NVEC, 128), F32),
        pltpu.VMEM((64, 128), F32),
        pltpu.VMEM((LEAVES, RANK, LINKS * RANK), BF16),
        pltpu.VMEM((LEAVES, NVEC, RANK), F32),
        pltpu.VMEM((NVEC, LEAVES * WIDTH), F32),
        dma,
        dma,
        dma((LEAVES,)),
        dma,
        dma((3,)),
        dma,
        dma,
        dma((2,)),
        dma,
        dma((2, 2)),
        dma,
        dma((2,)),
        dma,
        dma((2,)),
        dma,
        dma((2,)),
        dma,
        dma,
        dma,
        dma,
        dma((2,)),
        dma((2,)),
        dma((2,)),
    ]
    return pl.pallas_call(
        kernel,
        out_shape=jax.ShapeDtypeStruct(vectors.shape, BF16),
        in_specs=[pl.BlockSpec(memory_space=pl.ANY)] * 9,
        out_specs=pl.BlockSpec(memory_space=pltpu.VMEM),
        scratch_shapes=scratch,
        compiler_params=pltpu.CompilerParams(
            collective_id=0, has_side_effects=True, vmem_limit_bytes=40 * 2**20
        ),
        name="product",
    )(*[
        pltpu.with_memory_space_constraint(a, pltpu.HBM)
        for a in (vectors, basis, near, transfer, tree, offset, far, top, root)
    ])


def solution(mesh):
    placed = (
        P(None, ("leaf", "sub")),
        P(("leaf", "sub"), None, None),
        P(("leaf", "sub"), None, None),
        P(("leaf", "sub"), None, None),
        P(("leaf", "sub"), None),
        P(("leaf", "sub"), None),
        P(("leaf", "sub"), None, None, None),
        P("leaf", None),
        P("leaf", None, None, None),
    )
    return jax.shard_map(
        shards, mesh=mesh, in_specs=placed, out_specs=P(None, ("leaf", "sub")), check_vma=False
    )
```

```python
import functools

import jax
import jax.numpy as jnp
from jax import lax
from jax.experimental import pallas as pl
from jax.experimental.pallas import tpu as pltpu
from jax.sharding import PartitionSpec as P

MESH = pl.DeviceIdType.MESH
F32 = jnp.float32
BF16 = jnp.bfloat16
NT = (((1,), (1,)), ((), ()))
TREES = 64
SUBS = 4
LEAVES = 8
LINKS = 8
NVEC = 8
RANK = 64
WIDTH = 256
HOMES = 32


def dot(a, b):
    return jnp.dot(a, b, preferred_element_type=F32)


def dot_nt(a, b):
    return lax.dot_general(a, b, NT, preferred_element_type=F32)


def iota(shape, dim):
    return lax.broadcasted_iota(jnp.int32, shape, dim)


def drain(ref, sem):
    pltpu.make_async_copy(ref, ref, sem).wait()


def mirror(leaf):
    return leaf + 14 - 4 * lax.rem(leaf // 2, 8)


def home_leaf(j):
    return (lax.rem(j, 8) // 2) * 16 + (j // 8) * 2 + lax.rem(j, 2)


def slot_of(tree):
    m = tree & 15
    late = m >> 3
    m = (m ^ (late * 14)) & 7
    j = ((m >> 1) << 3) + ((tree >> 4) << 1) + (m & 1)
    return (late * HOMES + j) & (2 * HOMES - 1)


def kernel(
    vec_hbm, basis_hbm, near_hbm, trans_hbm, tree_hbm, offset_hbm, far_hbm, top_hbm, root_hbm,
    out_ref,
    x_v, basis_v, near_v, trans_v, tree_v, offset_v, far_v, root_v, top_v, slot_v, top_slot_v, client_v,
    slot_s, top_slot_s, client_s,
    table_send, table_recv, coef_send, coef_recv, part_send, part_recv, wide_v, both_v, plan_v,
    node_send, node_recv, node_mine, node_theirs, halo_v,
    reply_send, reply_recv, picked_v, rank_v, pairs_v, down_v, local_v,
    sem_x, sem_basis, sem_near, sem_trans, sem_table, sem_far, sem_root, sem_smem,
    halo_ssem, halo_rsem, table_ssem, table_rsem, coef_ssem, coef_rsem, part_ssem, part_rsem,
    node_ssem, node_rsem, reply_ssem, reply_rsem, fwd_sem, pick_sem, client_sem, pass_sem,
):
    me = lax.axis_index("leaf")
    sub = lax.axis_index("sub")
    late = lax.rem(me, 16) // 8
    other = mirror(me)
    home = me + late * (other - me)
    j = (lax.rem(home, 16) // 2) * 8 + (home // 16) * 2 + lax.rem(home, 2)
    row = j - lax.rem(j, 8)

    def step(leaf, s, by):
        flat = lax.rem(leaf * SUBS + s + by + TREES * SUBS, TREES * SUBS)
        return flat // SUBS, lax.rem(flat, SUBS)

    def home_of(leaf):
        late = lax.rem(leaf, 16) // 8
        return leaf + late * (mirror(leaf) - leaf), late

    barrier = pltpu.get_barrier_semaphore()

    def announce(leaf, s):
        pl.semaphore_signal(
            barrier, inc=1, device_id={"leaf": leaf, "sub": s}, device_id_type=MESH
        )

    def send(src, dst, ssem, rsem, leaf, s):
        pltpu.make_async_remote_copy(
            src_ref=src, dst_ref=dst, send_sem=ssem, recv_sem=rsem,
            device_id={"leaf": leaf, "sub": s}, device_id_type=MESH,
        ).start()

    @pl.when(late == 0)
    def _():
        def greet_late(i, carry):
            y, c = lax.rem(i, 8) // 2, lax.rem(i, 2)
            announce(lax.rem(me // 16 + y, 4) * 16 + (7 - i // 8) * 2 + c, sub)
            return carry

        def greet(i, carry):
            announce(home_leaf(lax.rem(j + i, HOMES)), sub)
            return carry

        for i in range(1, SUBS):
            announce(other, lax.rem(sub + i, SUBS))
        for leaf in (me, other):
            for by in (-1, 1):
                announce(*step(leaf, sub, by))
        lax.fori_loop(0, HOMES, greet_late, 0, unroll=True)
        lax.fori_loop(1, HOMES, greet, 0, unroll=True)

    @pl.when(late == 1)
    def _():
        for i in range(1, 4):
            announce(mirror(home_leaf(lax.rem(j + 8 * i, HOMES))), sub)
        for i in range(1, 8):
            announce(mirror(home_leaf(row + lax.rem(j + i, 8))), sub)

    for i in range(1, SUBS):
        announce(me, lax.rem(sub + i, SUBS))

    get_tree = pltpu.make_async_copy(tree_hbm, tree_v, sem_table.at[0])
    get_offset = pltpu.make_async_copy(offset_hbm, offset_v, sem_table.at[1])
    get_top = pltpu.make_async_copy(top_hbm, top_v, sem_table.at[2])
    get_x = pltpu.make_async_copy(vec_hbm, x_v, sem_x)
    get_basis = pltpu.make_async_copy(basis_hbm, basis_v, sem_basis)
    get_trans = pltpu.make_async_copy(trans_hbm, trans_v, sem_trans)
    get_far = pltpu.make_async_copy(far_hbm, far_v, sem_far)
    get_root = pltpu.make_async_copy(root_hbm, root_v, sem_root)
    get_near = [
        pltpu.make_async_copy(near_hbm.at[l], near_v.at[l], sem_near.at[l]) for l in range(LEAVES)
    ]
    for copy in (get_tree, get_offset, get_top, get_x, get_basis, get_trans):
        copy.start()
    get_far.start()
    get_root.start()
    for copy in get_near:
        copy.start()

    get_tree.wait()
    get_offset.wait()
    get_top.wait()
    slot_v[...] = slot_of(tree_v[...])
    top_slot_v[...] = slot_of(top_v[...])
    get_slot = pltpu.make_async_copy(slot_v, slot_s, sem_smem.at[0])
    get_top_slot = pltpu.make_async_copy(top_slot_v, top_slot_s, sem_smem.at[1])
    get_slot.start()
    get_top_slot.start()
    tree = tree_v[...].astype(F32).astype(BF16)
    offset = offset_v[...].astype(F32).astype(BF16)
    lane = iota((LINKS, 128), 1)
    column = iota((LINKS, 128), 0)
    low = jnp.where((lax.rem(lane, LINKS) == column) & (lane < 64), 1.0, 0.0).astype(BF16)
    rows = dot(tree, low) * 32.0 + dot(offset, low)
    own_row = lane // LINKS == column
    table_row = jnp.sum(jnp.where(own_row, rows, 0.0), axis=0, keepdims=True)
    table_row = table_row.astype(jnp.int32)
    table_send[...] = table_row

    get_x.wait()
    get_basis.wait()
    coefs = [
        dot_nt(x_v[:, l * WIDTH : (l + 1) * WIDTH], basis_v[l]).astype(BF16) for l in range(LEAVES)
    ]
    for l in range(0, LEAVES, 2):
        coef_send[l // 2] = jnp.concatenate(
            [coefs[l].astype(F32), coefs[l + 1].astype(F32)], axis=1
        ).astype(BF16)
    get_trans.wait()
    terms = [dot(coefs[l], trans_v[l]) for l in range(LEAVES)]
    partial = functools.reduce(jnp.add, terms)
    part_send[...] = jnp.concatenate([partial[0 : NVEC // 2], partial[NVEC // 2 :]], axis=1)

    def send_part(leaf, s):
        send(part_send, part_recv.at[late, sub], part_ssem, part_rsem.at[late], leaf, s)

    def send_coefs(leaf, s):
        send(coef_send, coef_recv.at[late * SUBS + sub], coef_ssem, coef_rsem.at[late], leaf, s)

    @pl.when(late == 0)
    def _():
        pl.semaphore_wait(barrier, HOMES - 1 + SUBS - 1 + 2)
        for i in range(1, SUBS):
            send_part(me, lax.rem(sub + i, SUBS))
        for i in range(1, SUBS):
            send_coefs(me, lax.rem(sub + i, SUBS))
        coef_recv[pl.ds(sub, 1)] = coef_send[...][None]
        part_recv[0, pl.ds(sub, 1)] = part_send[...][None]

    @pl.when(late == 1)
    def _():
        pl.semaphore_wait(barrier, HOMES + 7 + 3 + 2 * (SUBS - 1) + 2)
        for i in range(SUBS):
            send_part(other, lax.rem(sub + i, SUBS))
        for i in range(SUBS):
            send_coefs(other, lax.rem(sub + i, SUBS))
        for i in range(1, SUBS):
            send(
                coef_send, coef_recv.at[SUBS + sub], coef_ssem, coef_rsem.at[1],
                me, lax.rem(sub + i, SUBS),
            )
        coef_recv[pl.ds(SUBS + sub, 1)] = coef_send[...][None]

    @pl.when(late == 0)
    def _():
        table_recv[pl.ds(j, 1)] = table_send[...][None]

        def ask(i, carry):
            leaf = home_leaf(lax.rem(j + i, HOMES))
            send(table_send, table_recv.at[j], table_ssem, table_rsem.at[0], leaf, sub)
            return carry

        lax.fori_loop(1, HOMES, ask, 0, unroll=True)

    @pl.when(late == 1)
    def _():
        def ask(i, carry):
            leaf = home_leaf(lax.rem(j + i, HOMES))
            send(table_send, table_recv.at[HOMES + j], table_ssem, table_rsem.at[1], leaf, sub)
            return carry

        send(top_slot_v, client_v, client_sem.at[0], client_sem.at[1], other, sub)
        for i in range(1, 8):
            leaf = mirror(home_leaf(row + lax.rem(j + i, 8)))
            send(table_send, table_recv.at[HOMES + j], table_ssem, table_rsem.at[1], leaf, sub)
        lax.fori_loop(0, HOMES, ask, 0)
        table_recv[pl.ds(HOMES + j, 1)] = table_send[...][None]

    for side, by, start in ((0, 1, (LEAVES - 1) * WIDTH), (1, -1, 0)):
        leaf, s = step(me, sub, by)
        leaf, kind = home_of(leaf)
        send(
            vec_hbm.at[:, pl.ds(start, WIDTH)], halo_v.at[kind, side],
            halo_ssem, halo_rsem.at[kind, side], leaf, s,
        )

    entry = iota((64, LINKS), 0)
    link = iota((64, LINKS), 1)
    pick_row = jnp.where(entry // LINKS == link, 1.0, 0.0).astype(BF16)
    by_entry = dot(pick_row, tree)
    tree_col = jnp.sum(
        jnp.where(lax.rem(entry, LINKS) == link, by_entry, 0.0), axis=1, keepdims=True
    )
    tree_row = (table_row[:, 0:64] >> 5).astype(F32)
    same = (tree_col == tree_row) & (iota((64, 64), 1) < iota((64, 64), 0))
    rank_col = jnp.sum(jnp.where(same, 1.0, 0.0), axis=1, keepdims=True)
    rank_v[...] = jnp.broadcast_to(rank_col, (64, 128))

    get_far.wait()
    for l in range(LEAVES):
        for f in range(0, LINKS, 2):
            pairs_v[l, :, f * RANK : (f + 2) * RANK] = jnp.concatenate(
                [far_v[l, f], far_v[l, f + 1]], axis=1
            )

    def near(l, before, after):
        middle = x_v[:, l * WIDTH : (l + 1) * WIDTH]
        span = jnp.concatenate([before, middle, after], axis=1)
        local_v[:, l * WIDTH : (l + 1) * WIDTH] = dot_nt(span, near_v[l])

    for l in range(1, LEAVES - 1):
        get_near[l].wait()
        near(l, x_v[:, (l - 1) * WIDTH : l * WIDTH], x_v[:, (l + 1) * WIDTH : (l + 2) * WIDTH])
    get_near[0].wait()
    get_near[LEAVES - 1].wait()
    get_root.wait()
    get_slot.wait()
    get_top_slot.wait()

    @pl.when(late == 1)
    def _():
        drain(table_recv.at[pl.ds(0, 7)], table_rsem.at[1])
        rows = table_recv.at[pl.ds(HOMES + row, 8)]
        for i in range(1, 4):
            leaf = mirror(home_leaf(lax.rem(j + 8 * i, HOMES)))
            send(rows, rows, pass_sem.at[0], pass_sem.at[1], leaf, sub)

    earlier = jnp.where(iota((64, 64), 0) < iota((64, 64), 1), 1.0, 0.0).astype(BF16)
    row_no = iota((HOMES, SUBS * LEAVES), 1) + 1

    def plan(kind, asker, tree_id):
        table = table_recv[asker * HOMES : (asker + 1) * HOMES, 0, :][:, 0:64]
        asked = (table >> 5) == tree_id
        pair = (table & 31) >> 1
        odd = table & 1
        order = dot(jnp.where(asked, 1.0, 0.0).astype(BF16), earlier)
        rows = (
            jnp.where(asked & (order == 0.0), (pair + 16 * odd + 1).astype(F32), 0.0),
            jnp.where(asked & (order == 1.0), (pair + 16 - 16 * odd + 1).astype(F32), 0.0),
        )
        plan_v[2 * asker + kind] = jnp.concatenate(
            [
                jnp.where(
                    jnp.sum(r, axis=1, keepdims=True).astype(jnp.int32) == row_no, 1.0, 0.0
                )
                for r in rows
            ],
            axis=0,
        ).astype(BF16)

    def fill(kind, asker):
        at = 2 * asker + kind
        left = iota((HOMES, 128), 1) < 64
        onehot = plan_v[at]
        boths = [dot(onehot, both_v[kind, v]) for v in range(NVEC)]
        for v in range(NVEC):
            picked_v[at, :, v, :] = jnp.where(left, boths[v][0:HOMES], boths[v][HOMES:])
        reply_send[at * HOMES : (at + 1) * HOMES] = picked_v[at].astype(BF16)

    def sums(kind):
        node = functools.reduce(jnp.add, [part_recv[kind, i] for i in range(SUBS)]).astype(BF16)
        node_send[kind] = node
        node_recv[pl.ds(kind * HOMES + j, 1)] = node[None]

    def unpack(kind):
        pairs = coef_recv[kind * SUBS : (kind + 1) * SUBS]
        wide_v[kind] = pairs.reshape(SUBS * LEAVES // 2, NVEC, 128).astype(F32)
        for v in range(NVEC):
            straight = wide_v[kind, :, v, :]
            turned = pltpu.roll(straight, 64, 1)
            both_v[kind, v] = jnp.concatenate([straight, turned], axis=0).astype(BF16)

    def spread_nodes(kind):
        def one(i, carry):
            leaf = home_leaf(lax.rem(j + i, HOMES))
            send(node_send.at[kind], node_recv.at[kind * HOMES + j], node_ssem, node_rsem, leaf, sub)
            return carry

        lax.fori_loop(1, HOMES, one, 0, unroll=True)

    def reply(kind, asker):
        def one(i, carry):
            to = lax.rem(j + i, HOMES)
            leaf = home_leaf(to)
            if asker:
                leaf = mirror(leaf)
            send(
                reply_send.at[(2 * asker + kind) * HOMES + to], reply_recv.at[kind * HOMES + j],
                reply_ssem, reply_rsem, leaf, sub,
            )
            return carry

        lax.fori_loop(0 if kind < asker else 1, HOMES, one, 0, unroll=True)
        if kind >= asker:
            reply_recv[pl.ds(kind * HOMES + j, 1)] = reply_send[
                pl.ds((2 * asker + kind) * HOMES + j, 1)
            ]

    def near_ends():
        zero = jnp.zeros((NVEC, WIDTH), BF16)
        first = (me == 0) & (sub == 0)
        last = (me == TREES - 1) & (sub == SUBS - 1)
        near(0, jnp.where(first, zero, halo_v[0, 0]), x_v[:, WIDTH : 2 * WIDTH])
        near(
            LEAVES - 1,
            x_v[:, (LEAVES - 2) * WIDTH : (LEAVES - 1) * WIDTH],
            jnp.where(last, zero, halo_v[0, 1]),
        )

    @pl.when(late == 0)
    def _():
        drain(part_recv.at[0, pl.ds(0, SUBS - 1)], part_rsem.at[0])
        sums(0)
        spread_nodes(0)
        drain(coef_recv.at[pl.ds(0, SUBS - 1)], coef_rsem.at[0])
        unpack(0)
        drain(table_recv.at[pl.ds(0, HOMES - 1)], table_rsem.at[0])
        plan(0, 0, me)
        plan(1, 0, other)
        fill(0, 0)
        reply(0, 0)
        drain(part_recv.at[1], part_rsem.at[1])
        sums(1)
        spread_nodes(1)
        drain(coef_recv.at[pl.ds(SUBS, SUBS)], coef_rsem.at[1])
        unpack(1)
        fill(1, 0)
        reply(1, 0)
        drain(table_recv.at[pl.ds(0, HOMES)], table_rsem.at[1])
        drain(client_v, client_sem.at[1])
        get_client = pltpu.make_async_copy(client_v, client_s, sem_smem.at[0])
        get_client.start()
        plan(0, 1, me)
        fill(0, 1)
        reply(0, 1)
        for kind in range(2):
            for side in range(2):
                drain(halo_v.at[kind, side], halo_rsem.at[kind, side])
        send(halo_v.at[1], halo_v.at[0], fwd_sem.at[0], fwd_sem.at[1], other, sub)
        near_ends()
        get_client.wait()
        drain(node_recv.at[pl.ds(0, 2 * HOMES - 2)], node_rsem)
        for f in range(LINKS):
            node_theirs[f] = node_recv[client_s[0, f]]
        send(node_theirs, node_mine, pick_sem.at[0], pick_sem.at[1], other, sub)
        for f in range(LINKS):
            node_mine[f] = node_recv[top_slot_s[0, f]]

    @pl.when(late == 1)
    def _():
        drain(coef_recv.at[pl.ds(0, SUBS - 1)], coef_rsem.at[1])
        unpack(1)
        drain(table_recv.at[pl.ds(0, 24)], pass_sem.at[1])
        plan(1, 1, me)
        fill(1, 1)
        reply(1, 1)
        drain(halo_v.at[0], fwd_sem.at[1])
        near_ends()
        drain(node_mine, pick_sem.at[1])

    terms = []
    for f in range(LINKS):
        n = node_mine[f].astype(F32)
        n = jnp.concatenate([n[:, 0:64], n[:, 64:128]], axis=0).astype(BF16)
        terms.append(dot_nt(n, root_v[0, f]))
    root_local = functools.reduce(jnp.add, terms)
    hi = root_local.astype(BF16)
    rest = root_local - hi.astype(F32)
    mid = rest.astype(BF16)
    lo = (rest - mid.astype(F32)).astype(BF16)
    three = jnp.concatenate([hi, mid, lo], axis=0)
    terms = [dot_nt(three, trans_v[l]) for l in range(LEAVES)]
    for l in range(LEAVES):
        t = terms[l]
        down_v[l] = t[0:NVEC] + t[NVEC : 2 * NVEC] + t[2 * NVEC : 3 * NVEC]

    @pl.when(late == 0)
    def _():
        drain(reply_recv.at[pl.ds(0, 2 * HOMES - 2)], reply_rsem)

    @pl.when(late == 1)
    def _():
        drain(reply_recv.at[pl.ds(0, 2 * HOMES - 1)], reply_rsem)

    left = iota((NVEC, 128), 1) < 64
    coefs = []
    for l in range(LEAVES):
        parts = []
        for f in range(0, LINKS, 2):
            halves = []
            for k in range(2):
                e = l * LINKS + f + k
                got = reply_recv[slot_s[l, f + k]].astype(F32)
                there = jnp.broadcast_to(rank_v[e : e + 1, :], (NVEC, 128)) == float(k)
                halves.append(jnp.where(there, got, pltpu.roll(got, 64, 1)))
            parts.append(jnp.where(left, halves[0], halves[1]))
        coefs.append(jnp.concatenate(parts, axis=1).astype(BF16))
    fars = [dot_nt(coefs[l], pairs_v[l]) for l in range(LEAVES)]
    downs = [(fars[l] + down_v[l]).astype(BF16) for l in range(LEAVES)]
    outs = [dot(downs[l], basis_v[l]) for l in range(LEAVES)]
    for l in range(LEAVES):
        here = slice(l * WIDTH, (l + 1) * WIDTH)
        out_ref[:, here] = (local_v[:, here] + outs[l]).astype(BF16)

    drain(halo_v.at[0], halo_ssem)

    @pl.when(late == 0)
    def _():
        drain(coef_recv.at[pl.ds(0, SUBS - 1)], coef_ssem)
        drain(part_recv.at[0, pl.ds(0, SUBS - 1)], part_ssem)
        drain(table_recv.at[pl.ds(0, HOMES - 1)], table_ssem)
        drain(node_recv.at[pl.ds(0, 2 * HOMES - 2)], node_ssem)
        drain(reply_send.at[pl.ds(0, 3 * HOMES - 2)], reply_ssem)
        drain(halo_v.at[1], fwd_sem.at[0])
        drain(node_theirs, pick_sem.at[0])

    @pl.when(late == 1)
    def _():
        drain(coef_recv.at[pl.ds(0, 2 * SUBS - 1)], coef_ssem)
        drain(part_recv.at[0], part_ssem)
        drain(table_recv.at[pl.ds(0, HOMES + 7)], table_ssem)
        drain(table_recv.at[pl.ds(0, 24)], pass_sem.at[0])
        drain(client_v, client_sem.at[0])
        drain(reply_send.at[pl.ds(0, HOMES - 1)], reply_ssem)


def shards(vectors, basis, near, transfer, tree, offset, far, top, root):
    dma = pltpu.SemaphoreType.DMA
    i32 = jnp.int32
    scratch = [
        pltpu.VMEM((NVEC, LEAVES * WIDTH), BF16),
        pltpu.VMEM((LEAVES, RANK, WIDTH), BF16),
        pltpu.VMEM((LEAVES, WIDTH, 3 * WIDTH), BF16),
        pltpu.VMEM((LEAVES, RANK, RANK), BF16),
        pltpu.VMEM((LEAVES, LINKS), i32),
        pltpu.VMEM((LEAVES, LINKS), i32),
        pltpu.VMEM((LEAVES, LINKS, RANK, RANK), BF16),
        pltpu.VMEM((1, LINKS, RANK, RANK), BF16),
        pltpu.VMEM((1, LINKS), i32),
        pltpu.VMEM((LEAVES, LINKS), i32),
        pltpu.VMEM((1, LINKS), i32),
        pltpu.VMEM((1, LINKS), i32),
        pltpu.SMEM((LEAVES, LINKS), i32),
        pltpu.SMEM((1, LINKS), i32),
        pltpu.SMEM((1, LINKS), i32),
        pltpu.VMEM((1, 128), i32),
        pltpu.VMEM((2 * HOMES, 1, 128), i32),
        pltpu.VMEM((LEAVES // 2, NVEC, 128), BF16),
        pltpu.VMEM((2 * SUBS, LEAVES // 2, NVEC, 128), BF16),
        pltpu.VMEM((NVEC // 2, 128), F32),
        pltpu.VMEM((2, SUBS, NVEC // 2, 128), F32),
        pltpu.VMEM((2, SUBS * LEAVES // 2, NVEC, 128), F32),
        pltpu.VMEM((2, NVEC, SUBS * LEAVES, 128), BF16),
        pltpu.VMEM((4, 2 * HOMES, SUBS * LEAVES), BF16),
        pltpu.VMEM((2, NVEC // 2, 128), BF16),
        pltpu.VMEM((2 * HOMES, NVEC // 2, 128), BF16),
        pltpu.VMEM((LINKS, NVEC // 2, 128), BF16),
        pltpu.VMEM((LINKS, NVEC // 2, 128), BF16),
        pltpu.VMEM((2, 2, NVEC, WIDTH), BF16),
        pltpu.VMEM((4 * HOMES, NVEC, 128), BF16),
        pltpu.VMEM((2 * HOMES, NVEC, 128), BF16),
        pltpu.VMEM((4, HOMES, NVEC, 128), F32),
        pltpu.VMEM((64, 128), F32),
        pltpu.VMEM((LEAVES, RANK, LINKS * RANK), BF16),
        pltpu.VMEM((LEAVES, NVEC, RANK), F32),
        pltpu.VMEM((NVEC, LEAVES * WIDTH), F32),
        dma,
        dma,
        dma((LEAVES,)),
        dma,
        dma((3,)),
        dma,
        dma,
        dma((2,)),
        dma,
        dma((2, 2)),
        dma,
        dma((2,)),
        dma,
        dma((2,)),
        dma,
        dma((2,)),
        dma,
        dma,
        dma,
        dma,
        dma((2,)),
        dma((2,)),
        dma((2,)),
        dma((2,)),
    ]
    return pl.pallas_call(
        kernel,
        out_shape=jax.ShapeDtypeStruct(vectors.shape, BF16),
        in_specs=[pl.BlockSpec(memory_space=pl.ANY)] * 9,
        out_specs=pl.BlockSpec(memory_space=pltpu.VMEM),
        scratch_shapes=scratch,
        compiler_params=pltpu.CompilerParams(
            collective_id=0, has_side_effects=True, vmem_limit_bytes=40 * 2**20
        ),
        name="product",
    )(*[
        pltpu.with_memory_space_constraint(a, pltpu.HBM)
        for a in (vectors, basis, near, transfer, tree, offset, far, top, root)
    ])


def solution(mesh):
    placed = (
        P(None, ("leaf", "sub")),
        P(("leaf", "sub"), None, None),
        P(("leaf", "sub"), None, None),
        P(("leaf", "sub"), None, None),
        P(("leaf", "sub"), None),
        P(("leaf", "sub"), None),
        P(("leaf", "sub"), None, None, None),
        P("leaf", None),
        P("leaf", None, None, None),
    )
    return jax.shard_map(
        shards, mesh=mesh, in_specs=placed, out_specs=P(None, ("leaf", "sub")), check_vma=False
    )
```

```python
import functools

import jax
import jax.numpy as jnp
from jax import lax
from jax.experimental import pallas as pl
from jax.experimental.pallas import tpu as pltpu
from jax.sharding import PartitionSpec as P

MESH = pl.DeviceIdType.MESH
F32 = jnp.float32
BF16 = jnp.bfloat16
NT = (((1,), (1,)), ((), ()))
TREES = 64
SUBS = 4
LEAVES = 8
LINKS = 8
NVEC = 8
RANK = 64
WIDTH = 256
HOMES = 32


def dot(a, b):
    return jnp.dot(a, b, preferred_element_type=F32)


def dot_nt(a, b):
    return lax.dot_general(a, b, NT, preferred_element_type=F32)


def iota(shape, dim):
    return lax.broadcasted_iota(jnp.int32, shape, dim)


def drain(ref, sem):
    pltpu.make_async_copy(ref, ref, sem).wait()


def mirror(leaf):
    return leaf + 14 - 4 * lax.rem(leaf // 2, 8)


def home_leaf(j):
    return (lax.rem(j, 8) // 2) * 16 + (j // 8) * 2 + lax.rem(j, 2)


def slot_of(tree):
    m = tree & 15
    late = m >> 3
    m = (m ^ (late * 14)) & 7
    j = ((m >> 1) << 3) + ((tree >> 4) << 1) + (m & 1)
    return (late * HOMES + j) & (2 * HOMES - 1)


def kernel(
    vec_hbm, basis_hbm, near_hbm, trans_hbm, tree_hbm, offset_hbm, far_hbm, top_hbm, root_hbm,
    out_ref,
    x_v, basis_v, near_v, trans_v, tree_v, offset_v, far_v, root_v, top_v, slot_v, top_slot_v, client_v,
    slot_s, top_slot_s, client_s,
    table_send, table_recv, coef_send, coef_recv, part_send, part_recv, wide_v, both_v, plan_v,
    node_send, node_recv, node_mine, node_theirs, halo_v,
    reply_send, reply_recv, picked_v, rank_v, pairs_v, down_v, local_v,
    sem_x, sem_basis, sem_near, sem_trans, sem_table, sem_far, sem_root, sem_smem,
    halo_ssem, halo_rsem, table_ssem, table_rsem, coef_ssem, coef_rsem, part_ssem, part_rsem,
    node_ssem, node_rsem, reply_ssem, reply_rsem, fwd_sem, pick_sem, client_sem, pass_sem,
):
    me = lax.axis_index("leaf")
    sub = lax.axis_index("sub")
    late = lax.rem(me, 16) // 8
    other = mirror(me)
    home = me + late * (other - me)
    j = (lax.rem(home, 16) // 2) * 8 + (home // 16) * 2 + lax.rem(home, 2)
    row = j - lax.rem(j, 8)

    def step(leaf, s, by):
        flat = lax.rem(leaf * SUBS + s + by + TREES * SUBS, TREES * SUBS)
        return flat // SUBS, lax.rem(flat, SUBS)

    def home_of(leaf):
        late = lax.rem(leaf, 16) // 8
        return leaf + late * (mirror(leaf) - leaf), late

    barrier = pltpu.get_barrier_semaphore()

    def announce(leaf, s):
        pl.semaphore_signal(
            barrier, inc=1, device_id={"leaf": leaf, "sub": s}, device_id_type=MESH
        )

    def send(src, dst, ssem, rsem, leaf, s):
        pltpu.make_async_remote_copy(
            src_ref=src, dst_ref=dst, send_sem=ssem, recv_sem=rsem,
            device_id={"leaf": leaf, "sub": s}, device_id_type=MESH,
        ).start()

    get_tree = pltpu.make_async_copy(tree_hbm, tree_v, sem_table.at[0])
    get_offset = pltpu.make_async_copy(offset_hbm, offset_v, sem_table.at[1])
    get_top = pltpu.make_async_copy(top_hbm, top_v, sem_table.at[2])
    get_x = pltpu.make_async_copy(vec_hbm, x_v, sem_x)
    get_basis = pltpu.make_async_copy(basis_hbm, basis_v, sem_basis)
    get_trans = pltpu.make_async_copy(trans_hbm, trans_v, sem_trans)
    get_far = pltpu.make_async_copy(far_hbm, far_v, sem_far)
    get_root = pltpu.make_async_copy(root_hbm, root_v, sem_root)
    get_near = [
        pltpu.make_async_copy(near_hbm.at[l], near_v.at[l], sem_near.at[l]) for l in range(LEAVES)
    ]
    now = (get_x, get_basis, get_trans, get_tree, get_offset, get_top)
    soon = (get_far, get_root, *get_near)

    @pl.when(late == 1)
    def _():
        for copy in now:
            copy.start()

    @pl.when(late == 0)
    def _():
        def greet_late(i, carry):
            y, c = lax.rem(i, 8) // 2, lax.rem(i, 2)
            announce(lax.rem(me // 16 + y, 4) * 16 + (7 - i // 8) * 2 + c, sub)
            return carry

        def greet(i, carry):
            announce(home_leaf(lax.rem(j + i, HOMES)), sub)
            return carry

        lax.fori_loop(0, 16, greet_late, 0, unroll=True)
        for i in range(1, SUBS):
            announce(other, lax.rem(sub + i, SUBS))
        for leaf in (me, other):
            for by in (-1, 1):
                announce(*step(leaf, sub, by))
        lax.fori_loop(1, HOMES, greet, 0, unroll=True)
        lax.fori_loop(16, HOMES, greet_late, 0, unroll=True)

    @pl.when(late == 1)
    def _():
        for i in range(1, 4):
            announce(mirror(home_leaf(lax.rem(j + 8 * i, HOMES))), sub)
        for i in range(1, 8):
            announce(mirror(home_leaf(row + lax.rem(j + i, 8))), sub)

    for i in range(1, SUBS):
        announce(me, lax.rem(sub + i, SUBS))

    @pl.when(late == 0)
    def _():
        for copy in (*now, *soon):
            copy.start()

    get_x.wait()
    get_basis.wait()
    coefs = [
        dot_nt(x_v[:, l * WIDTH : (l + 1) * WIDTH], basis_v[l]).astype(BF16) for l in range(LEAVES)
    ]
    for l in range(0, LEAVES, 2):
        coef_send[l // 2] = jnp.concatenate(
            [coefs[l].astype(F32), coefs[l + 1].astype(F32)], axis=1
        ).astype(BF16)
    get_trans.wait()
    terms = [dot(coefs[l], trans_v[l]) for l in range(LEAVES)]
    partial = functools.reduce(jnp.add, terms)
    part_send[...] = jnp.concatenate([partial[0 : NVEC // 2], partial[NVEC // 2 :]], axis=1)

    def send_part(leaf, s):
        send(part_send, part_recv.at[late, sub], part_ssem, part_rsem.at[late], leaf, s)

    def send_coefs(leaf, s):
        send(coef_send, coef_recv.at[late * SUBS + sub], coef_ssem, coef_rsem.at[late], leaf, s)

    @pl.when(late == 0)
    def _():
        pl.semaphore_wait(barrier, HOMES - 1 + SUBS - 1 + 2)
        for i in range(1, SUBS):
            send_part(me, lax.rem(sub + i, SUBS))
        for i in range(1, SUBS):
            send_coefs(me, lax.rem(sub + i, SUBS))
        coef_recv[pl.ds(sub, 1)] = coef_send[...][None]
        part_recv[0, pl.ds(sub, 1)] = part_send[...][None]

    @pl.when(late == 1)
    def _():
        pl.semaphore_wait(barrier, HOMES + 7 + 3 + 2 * (SUBS - 1) + 2)
        for i in range(SUBS):
            send_part(other, lax.rem(sub + i, SUBS))
        for i in range(SUBS):
            send_coefs(other, lax.rem(sub + i, SUBS))
        for i in range(1, SUBS):
            send(
                coef_send, coef_recv.at[SUBS + sub], coef_ssem, coef_rsem.at[1],
                me, lax.rem(sub + i, SUBS),
            )
        coef_recv[pl.ds(SUBS + sub, 1)] = coef_send[...][None]

    get_tree.wait()
    get_offset.wait()
    get_top.wait()
    slot_v[...] = slot_of(tree_v[...])
    top_slot_v[...] = slot_of(top_v[...])
    get_slot = pltpu.make_async_copy(slot_v, slot_s, sem_smem.at[0])
    get_top_slot = pltpu.make_async_copy(top_slot_v, top_slot_s, sem_smem.at[1])
    get_slot.start()
    get_top_slot.start()
    tree = tree_v[...].astype(F32).astype(BF16)
    offset = offset_v[...].astype(F32).astype(BF16)
    lane = iota((LINKS, 128), 1)
    column = iota((LINKS, 128), 0)
    low = jnp.where((lax.rem(lane, LINKS) == column) & (lane < 64), 1.0, 0.0).astype(BF16)
    rows = dot(tree, low) * 32.0 + dot(offset, low)
    own_row = lane // LINKS == column
    table_row = jnp.sum(jnp.where(own_row, rows, 0.0), axis=0, keepdims=True)
    table_row = table_row.astype(jnp.int32)
    table_send[...] = table_row

    @pl.when(late == 0)
    def _():
        table_recv[pl.ds(j, 1)] = table_send[...][None]

        def ask(i, carry):
            leaf = home_leaf(lax.rem(j + i, HOMES))
            send(table_send, table_recv.at[j], table_ssem, table_rsem.at[0], leaf, sub)
            return carry

        lax.fori_loop(1, HOMES, ask, 0, unroll=True)

    @pl.when(late == 1)
    def _():
        def ask(i, carry):
            leaf = home_leaf(lax.rem(j + i, HOMES))
            send(table_send, table_recv.at[HOMES + j], table_ssem, table_rsem.at[1], leaf, sub)
            return carry

        send(top_slot_v, client_v, client_sem.at[0], client_sem.at[1], other, sub)
        for i in range(1, 8):
            leaf = mirror(home_leaf(row + lax.rem(j + i, 8)))
            send(table_send, table_recv.at[HOMES + j], table_ssem, table_rsem.at[1], leaf, sub)
        lax.fori_loop(0, HOMES, ask, 0)
        table_recv[pl.ds(HOMES + j, 1)] = table_send[...][None]

    for side, by, start in ((0, 1, (LEAVES - 1) * WIDTH), (1, -1, 0)):
        leaf, s = step(me, sub, by)
        leaf, kind = home_of(leaf)
        send(
            vec_hbm.at[:, pl.ds(start, WIDTH)], halo_v.at[kind, side],
            halo_ssem, halo_rsem.at[kind, side], leaf, s,
        )

    @pl.when(late == 1)
    def _():
        for copy in soon:
            copy.start()

    entry = iota((64, LINKS), 0)
    link = iota((64, LINKS), 1)
    pick_row = jnp.where(entry // LINKS == link, 1.0, 0.0).astype(BF16)
    by_entry = dot(pick_row, tree)
    tree_col = jnp.sum(
        jnp.where(lax.rem(entry, LINKS) == link, by_entry, 0.0), axis=1, keepdims=True
    )
    tree_row = (table_row[:, 0:64] >> 5).astype(F32)
    same = (tree_col == tree_row) & (iota((64, 64), 1) < iota((64, 64), 0))
    rank_col = jnp.sum(jnp.where(same, 1.0, 0.0), axis=1, keepdims=True)
    rank_v[...] = jnp.broadcast_to(rank_col, (64, 128))

    get_far.wait()
    for l in range(LEAVES):
        for f in range(0, LINKS, 2):
            pairs_v[l, :, f * RANK : (f + 2) * RANK] = jnp.concatenate(
                [far_v[l, f], far_v[l, f + 1]], axis=1
            )

    def near(l, before, after):
        middle = x_v[:, l * WIDTH : (l + 1) * WIDTH]
        span = jnp.concatenate([before, middle, after], axis=1)
        local_v[:, l * WIDTH : (l + 1) * WIDTH] = dot_nt(span, near_v[l])

    for l in range(1, LEAVES - 1):
        get_near[l].wait()
        near(l, x_v[:, (l - 1) * WIDTH : l * WIDTH], x_v[:, (l + 1) * WIDTH : (l + 2) * WIDTH])
    get_near[0].wait()
    get_near[LEAVES - 1].wait()
    get_root.wait()
    get_slot.wait()
    get_top_slot.wait()

    @pl.when(late == 1)
    def _():
        drain(table_recv.at[pl.ds(0, 7)], table_rsem.at[1])
        rows = table_recv.at[pl.ds(HOMES + row, 8)]
        for i in range(1, 4):
            leaf = mirror(home_leaf(lax.rem(j + 8 * i, HOMES)))
            send(rows, rows, pass_sem.at[0], pass_sem.at[1], leaf, sub)

    earlier = jnp.where(iota((64, 64), 0) < iota((64, 64), 1), 1.0, 0.0).astype(BF16)
    row_no = iota((HOMES, SUBS * LEAVES), 1) + 1

    def plan(kind, asker, tree_id):
        table = table_recv[asker * HOMES : (asker + 1) * HOMES, 0, :][:, 0:64]
        asked = (table >> 5) == tree_id
        pair = (table & 31) >> 1
        odd = table & 1
        order = dot(jnp.where(asked, 1.0, 0.0).astype(BF16), earlier)
        rows = (
            jnp.where(asked & (order == 0.0), (pair + 16 * odd + 1).astype(F32), 0.0),
            jnp.where(asked & (order == 1.0), (pair + 16 - 16 * odd + 1).astype(F32), 0.0),
        )
        plan_v[2 * asker + kind] = jnp.concatenate(
            [
                jnp.where(
                    jnp.sum(r, axis=1, keepdims=True).astype(jnp.int32) == row_no, 1.0, 0.0
                )
                for r in rows
            ],
            axis=0,
        ).astype(BF16)

    def fill(kind, asker):
        at = 2 * asker + kind
        left = iota((HOMES, 128), 1) < 64
        onehot = plan_v[at]
        boths = [dot(onehot, both_v[kind, v]) for v in range(NVEC)]
        for v in range(NVEC):
            picked_v[at, :, v, :] = jnp.where(left, boths[v][0:HOMES], boths[v][HOMES:])
        reply_send[at * HOMES : (at + 1) * HOMES] = picked_v[at].astype(BF16)

    def sums(kind):
        node = functools.reduce(jnp.add, [part_recv[kind, i] for i in range(SUBS)]).astype(BF16)
        node_send[kind] = node
        node_recv[pl.ds(kind * HOMES + j, 1)] = node[None]

    def unpack(kind):
        pairs = coef_recv[kind * SUBS : (kind + 1) * SUBS]
        wide_v[kind] = pairs.reshape(SUBS * LEAVES // 2, NVEC, 128).astype(F32)
        for v in range(NVEC):
            straight = wide_v[kind, :, v, :]
            turned = pltpu.roll(straight, 64, 1)
            both_v[kind, v] = jnp.concatenate([straight, turned], axis=0).astype(BF16)

    def spread_nodes(kind):
        def one(i, carry):
            leaf = home_leaf(lax.rem(j + i, HOMES))
            send(node_send.at[kind], node_recv.at[kind * HOMES + j], node_ssem, node_rsem, leaf, sub)
            return carry

        lax.fori_loop(1, HOMES, one, 0, unroll=True)

    def reply(kind, asker):
        def one(i, carry):
            to = lax.rem(j + i, HOMES)
            leaf = home_leaf(to)
            if asker:
                leaf = mirror(leaf)
            send(
                reply_send.at[(2 * asker + kind) * HOMES + to], reply_recv.at[kind * HOMES + j],
                reply_ssem, reply_rsem, leaf, sub,
            )
            return carry

        lax.fori_loop(0 if kind < asker else 1, HOMES, one, 0, unroll=True)
        if kind >= asker:
            reply_recv[pl.ds(kind * HOMES + j, 1)] = reply_send[
                pl.ds((2 * asker + kind) * HOMES + j, 1)
            ]

    def near_ends():
        zero = jnp.zeros((NVEC, WIDTH), BF16)
        first = (me == 0) & (sub == 0)
        last = (me == TREES - 1) & (sub == SUBS - 1)
        near(0, jnp.where(first, zero, halo_v[0, 0]), x_v[:, WIDTH : 2 * WIDTH])
        near(
            LEAVES - 1,
            x_v[:, (LEAVES - 2) * WIDTH : (LEAVES - 1) * WIDTH],
            jnp.where(last, zero, halo_v[0, 1]),
        )

    @pl.when(late == 0)
    def _():
        drain(part_recv.at[0, pl.ds(0, SUBS - 1)], part_rsem.at[0])
        sums(0)
        spread_nodes(0)
        drain(coef_recv.at[pl.ds(0, SUBS - 1)], coef_rsem.at[0])
        unpack(0)
        drain(table_recv.at[pl.ds(0, HOMES - 1)], table_rsem.at[0])
        plan(0, 0, me)
        plan(1, 0, other)
        fill(0, 0)
        reply(0, 0)
        drain(part_recv.at[1], part_rsem.at[1])
        sums(1)
        spread_nodes(1)
        drain(coef_recv.at[pl.ds(SUBS, SUBS)], coef_rsem.at[1])
        unpack(1)
        fill(1, 0)
        reply(1, 0)
        drain(table_recv.at[pl.ds(0, HOMES)], table_rsem.at[1])
        drain(client_v, client_sem.at[1])
        get_client = pltpu.make_async_copy(client_v, client_s, sem_smem.at[0])
        get_client.start()
        plan(0, 1, me)
        fill(0, 1)
        reply(0, 1)
        for kind in range(2):
            for side in range(2):
                drain(halo_v.at[kind, side], halo_rsem.at[kind, side])
        send(halo_v.at[1], halo_v.at[0], fwd_sem.at[0], fwd_sem.at[1], other, sub)
        near_ends()
        get_client.wait()
        drain(node_recv.at[pl.ds(0, 2 * HOMES - 2)], node_rsem)
        for f in range(LINKS):
            node_theirs[f] = node_recv[client_s[0, f]]
        send(node_theirs, node_mine, pick_sem.at[0], pick_sem.at[1], other, sub)
        for f in range(LINKS):
            node_mine[f] = node_recv[top_slot_s[0, f]]

    @pl.when(late == 1)
    def _():
        drain(coef_recv.at[pl.ds(0, SUBS - 1)], coef_rsem.at[1])
        unpack(1)
        drain(table_recv.at[pl.ds(0, 24)], pass_sem.at[1])
        plan(1, 1, me)
        fill(1, 1)
        reply(1, 1)
        drain(halo_v.at[0], fwd_sem.at[1])
        near_ends()
        drain(node_mine, pick_sem.at[1])

    terms = []
    for f in range(LINKS):
        n = node_mine[f].astype(F32)
        n = jnp.concatenate([n[:, 0:64], n[:, 64:128]], axis=0).astype(BF16)
        terms.append(dot_nt(n, root_v[0, f]))
    root_local = functools.reduce(jnp.add, terms)
    hi = root_local.astype(BF16)
    rest = root_local - hi.astype(F32)
    mid = rest.astype(BF16)
    lo = (rest - mid.astype(F32)).astype(BF16)
    three = jnp.concatenate([hi, mid, lo], axis=0)
    terms = [dot_nt(three, trans_v[l]) for l in range(LEAVES)]
    for l in range(LEAVES):
        t = terms[l]
        down_v[l] = t[0:NVEC] + t[NVEC : 2 * NVEC] + t[2 * NVEC : 3 * NVEC]

    @pl.when(late == 0)
    def _():
        drain(reply_recv.at[pl.ds(0, 2 * HOMES - 2)], reply_rsem)

    @pl.when(late == 1)
    def _():
        drain(reply_recv.at[pl.ds(0, 2 * HOMES - 1)], reply_rsem)

    left = iota((NVEC, 128), 1) < 64
    coefs = []
    for l in range(LEAVES):
        parts = []
        for f in range(0, LINKS, 2):
            halves = []
            for k in range(2):
                e = l * LINKS + f + k
                got = reply_recv[slot_s[l, f + k]].astype(F32)
                there = jnp.broadcast_to(rank_v[e : e + 1, :], (NVEC, 128)) == float(k)
                halves.append(jnp.where(there, got, pltpu.roll(got, 64, 1)))
            parts.append(jnp.where(left, halves[0], halves[1]))
        coefs.append(jnp.concatenate(parts, axis=1).astype(BF16))
    fars = [dot_nt(coefs[l], pairs_v[l]) for l in range(LEAVES)]
    downs = [(fars[l] + down_v[l]).astype(BF16) for l in range(LEAVES)]
    outs = [dot(downs[l], basis_v[l]) for l in range(LEAVES)]
    for l in range(LEAVES):
        here = slice(l * WIDTH, (l + 1) * WIDTH)
        out_ref[:, here] = (local_v[:, here] + outs[l]).astype(BF16)

    drain(halo_v.at[0], halo_ssem)

    @pl.when(late == 0)
    def _():
        drain(coef_recv.at[pl.ds(0, SUBS - 1)], coef_ssem)
        drain(part_recv.at[0, pl.ds(0, SUBS - 1)], part_ssem)
        drain(table_recv.at[pl.ds(0, HOMES - 1)], table_ssem)
        drain(node_recv.at[pl.ds(0, 2 * HOMES - 2)], node_ssem)
        drain(reply_send.at[pl.ds(0, 3 * HOMES - 2)], reply_ssem)
        drain(halo_v.at[1], fwd_sem.at[0])
        drain(node_theirs, pick_sem.at[0])

    @pl.when(late == 1)
    def _():
        drain(coef_recv.at[pl.ds(0, 2 * SUBS - 1)], coef_ssem)
        drain(part_recv.at[0], part_ssem)
        drain(table_recv.at[pl.ds(0, HOMES + 7)], table_ssem)
        drain(table_recv.at[pl.ds(0, 24)], pass_sem.at[0])
        drain(client_v, client_sem.at[0])
        drain(reply_send.at[pl.ds(0, HOMES - 1)], reply_ssem)


def shards(vectors, basis, near, transfer, tree, offset, far, top, root):
    dma = pltpu.SemaphoreType.DMA
    i32 = jnp.int32
    scratch = [
        pltpu.VMEM((NVEC, LEAVES * WIDTH), BF16),
        pltpu.VMEM((LEAVES, RANK, WIDTH), BF16),
        pltpu.VMEM((LEAVES, WIDTH, 3 * WIDTH), BF16),
        pltpu.VMEM((LEAVES, RANK, RANK), BF16),
        pltpu.VMEM((LEAVES, LINKS), i32),
        pltpu.VMEM((LEAVES, LINKS), i32),
        pltpu.VMEM((LEAVES, LINKS, RANK, RANK), BF16),
        pltpu.VMEM((1, LINKS, RANK, RANK), BF16),
        pltpu.VMEM((1, LINKS), i32),
        pltpu.VMEM((LEAVES, LINKS), i32),
        pltpu.VMEM((1, LINKS), i32),
        pltpu.VMEM((1, LINKS), i32),
        pltpu.SMEM((LEAVES, LINKS), i32),
        pltpu.SMEM((1, LINKS), i32),
        pltpu.SMEM((1, LINKS), i32),
        pltpu.VMEM((1, 128), i32),
        pltpu.VMEM((2 * HOMES, 1, 128), i32),
        pltpu.VMEM((LEAVES // 2, NVEC, 128), BF16),
        pltpu.VMEM((2 * SUBS, LEAVES // 2, NVEC, 128), BF16),
        pltpu.VMEM((NVEC // 2, 128), F32),
        pltpu.VMEM((2, SUBS, NVEC // 2, 128), F32),
        pltpu.VMEM((2, SUBS * LEAVES // 2, NVEC, 128), F32),
        pltpu.VMEM((2, NVEC, SUBS * LEAVES, 128), BF16),
        pltpu.VMEM((4, 2 * HOMES, SUBS * LEAVES), BF16),
        pltpu.VMEM((2, NVEC // 2, 128), BF16),
        pltpu.VMEM((2 * HOMES, NVEC // 2, 128), BF16),
        pltpu.VMEM((LINKS, NVEC // 2, 128), BF16),
        pltpu.VMEM((LINKS, NVEC // 2, 128), BF16),
        pltpu.VMEM((2, 2, NVEC, WIDTH), BF16),
        pltpu.VMEM((4 * HOMES, NVEC, 128), BF16),
        pltpu.VMEM((2 * HOMES, NVEC, 128), BF16),
        pltpu.VMEM((4, HOMES, NVEC, 128), F32),
        pltpu.VMEM((64, 128), F32),
        pltpu.VMEM((LEAVES, RANK, LINKS * RANK), BF16),
        pltpu.VMEM((LEAVES, NVEC, RANK), F32),
        pltpu.VMEM((NVEC, LEAVES * WIDTH), F32),
        dma,
        dma,
        dma((LEAVES,)),
        dma,
        dma((3,)),
        dma,
        dma,
        dma((2,)),
        dma,
        dma((2, 2)),
        dma,
        dma((2,)),
        dma,
        dma((2,)),
        dma,
        dma((2,)),
        dma,
        dma,
        dma,
        dma,
        dma((2,)),
        dma((2,)),
        dma((2,)),
        dma((2,)),
    ]
    return pl.pallas_call(
        kernel,
        out_shape=jax.ShapeDtypeStruct(vectors.shape, BF16),
        in_specs=[pl.BlockSpec(memory_space=pl.ANY)] * 9,
        out_specs=pl.BlockSpec(memory_space=pltpu.VMEM),
        scratch_shapes=scratch,
        compiler_params=pltpu.CompilerParams(
            collective_id=0, has_side_effects=True, vmem_limit_bytes=40 * 2**20
        ),
        name="product",
    )(*[
        pltpu.with_memory_space_constraint(a, pltpu.HBM)
        for a in (vectors, basis, near, transfer, tree, offset, far, top, root)
    ])


def solution(mesh):
    placed = (
        P(None, ("leaf", "sub")),
        P(("leaf", "sub"), None, None),
        P(("leaf", "sub"), None, None),
        P(("leaf", "sub"), None, None),
        P(("leaf", "sub"), None),
        P(("leaf", "sub"), None),
        P(("leaf", "sub"), None, None, None),
        P("leaf", None),
        P("leaf", None, None, None),
    )
    return jax.shard_map(
        shards, mesh=mesh, in_specs=placed, out_specs=P(None, ("leaf", "sub")), check_vma=False
    )
```

```python
import functools

import jax
import jax.numpy as jnp
from jax import lax
from jax.experimental import pallas as pl
from jax.experimental.pallas import tpu as pltpu
from jax.sharding import PartitionSpec as P

MESH = pl.DeviceIdType.MESH
F32 = jnp.float32
BF16 = jnp.bfloat16
NT = (((1,), (1,)), ((), ()))
TREES = 64
SUBS = 4
LEAVES = 8
LINKS = 8
NVEC = 8
RANK = 64
WIDTH = 256
HOMES = 32


def dot(a, b):
    return jnp.dot(a, b, preferred_element_type=F32)


def dot_nt(a, b):
    return lax.dot_general(a, b, NT, preferred_element_type=F32)


def iota(shape, dim):
    return lax.broadcasted_iota(jnp.int32, shape, dim)


def drain(ref, sem):
    pltpu.make_async_copy(ref, ref, sem).wait()


def mirror(leaf):
    return leaf + 14 - 4 * lax.rem(leaf // 2, 8)


def home_leaf(j):
    return (lax.rem(j, 8) // 2) * 16 + (j // 8) * 2 + lax.rem(j, 2)


def slot_of(tree):
    m = tree & 15
    late = m >> 3
    m = (m ^ (late * 14)) & 7
    j = ((m >> 1) << 3) + ((tree >> 4) << 1) + (m & 1)
    return (late * HOMES + j) & (2 * HOMES - 1)


def kernel(
    vec_hbm, basis_hbm, near_hbm, trans_hbm, tree_hbm, offset_hbm, far_hbm, top_hbm, root_hbm,
    out_ref,
    x_v, basis_v, near_v, trans_v, tree_v, offset_v, far_v, root_v, top_v, slot_v, top_slot_v, client_v,
    slot_s, top_slot_s, client_s,
    table_send, table_recv, coef_send, coef_recv, part_send, part_recv, wide_v, both_v, plan_v,
    node_send, node_recv, node_mine, node_theirs, halo_v,
    reply_send, reply_recv, picked_v, rank_v, pairs_v, root_pairs_v, down_v, local_v,
    sem_x, sem_basis, sem_near, sem_trans, sem_table, sem_far, sem_root, sem_smem,
    halo_ssem, halo_rsem, table_ssem, table_rsem, coef_ssem, coef_rsem, part_ssem, part_rsem,
    node_ssem, node_rsem, reply_ssem, reply_rsem, fwd_sem, pick_sem, client_sem, pass_sem,
):
    me = lax.axis_index("leaf")
    sub = lax.axis_index("sub")
    late = lax.rem(me, 16) // 8
    other = mirror(me)
    home = me + late * (other - me)
    j = (lax.rem(home, 16) // 2) * 8 + (home // 16) * 2 + lax.rem(home, 2)
    row = j - lax.rem(j, 8)

    def step(leaf, s, by):
        flat = lax.rem(leaf * SUBS + s + by + TREES * SUBS, TREES * SUBS)
        return flat // SUBS, lax.rem(flat, SUBS)

    def home_of(leaf):
        late = lax.rem(leaf, 16) // 8
        return leaf + late * (mirror(leaf) - leaf), late

    barrier = pltpu.get_barrier_semaphore()

    def announce(leaf, s):
        pl.semaphore_signal(
            barrier, inc=1, device_id={"leaf": leaf, "sub": s}, device_id_type=MESH
        )

    def send(src, dst, ssem, rsem, leaf, s):
        pltpu.make_async_remote_copy(
            src_ref=src, dst_ref=dst, send_sem=ssem, recv_sem=rsem,
            device_id={"leaf": leaf, "sub": s}, device_id_type=MESH,
        ).start()

    @pl.when(late == 0)
    def _():
        def greet_late(i, carry):
            y, c = lax.rem(i, 8) // 2, lax.rem(i, 2)
            announce(lax.rem(me // 16 + y, 4) * 16 + (7 - i // 8) * 2 + c, sub)
            return carry

        def greet(i, carry):
            announce(home_leaf(lax.rem(j + i, HOMES)), sub)
            return carry

        for i in range(1, SUBS):
            announce(other, lax.rem(sub + i, SUBS))
        for leaf in (me, other):
            for by in (-1, 1):
                announce(*step(leaf, sub, by))
        lax.fori_loop(0, 16, greet_late, 0, unroll=True)
        lax.fori_loop(1, HOMES, greet, 0, unroll=True)
        lax.fori_loop(16, HOMES, greet_late, 0, unroll=True)

    @pl.when(late == 1)
    def _():
        for i in range(1, 4):
            announce(mirror(home_leaf(lax.rem(j + 8 * i, HOMES))), sub)
        for i in range(1, 8):
            announce(mirror(home_leaf(row + lax.rem(j + i, 8))), sub)

    for i in range(1, SUBS):
        announce(me, lax.rem(sub + i, SUBS))

    get_tree = pltpu.make_async_copy(tree_hbm, tree_v, sem_table.at[0])
    get_offset = pltpu.make_async_copy(offset_hbm, offset_v, sem_table.at[1])
    get_top = pltpu.make_async_copy(top_hbm, top_v, sem_table.at[2])
    get_x = pltpu.make_async_copy(vec_hbm, x_v, sem_x)
    get_basis = pltpu.make_async_copy(basis_hbm, basis_v, sem_basis)
    get_trans = pltpu.make_async_copy(trans_hbm, trans_v, sem_trans)
    get_far = pltpu.make_async_copy(far_hbm, far_v, sem_far)
    get_root = pltpu.make_async_copy(root_hbm, root_v, sem_root)
    get_near = [
        pltpu.make_async_copy(near_hbm.at[l], near_v.at[l], sem_near.at[l]) for l in range(LEAVES)
    ]
    for copy in (get_tree, get_offset, get_top, get_x, get_basis, get_trans):
        copy.start()
    get_far.start()
    get_root.start()
    for copy in get_near:
        copy.start()

    get_tree.wait()
    get_offset.wait()
    get_top.wait()
    slot_v[...] = slot_of(tree_v[...])
    top_slot_v[...] = slot_of(top_v[...])
    get_slot = pltpu.make_async_copy(slot_v, slot_s, sem_smem.at[0])
    get_top_slot = pltpu.make_async_copy(top_slot_v, top_slot_s, sem_smem.at[1])
    get_slot.start()
    get_top_slot.start()
    tree = tree_v[...].astype(F32).astype(BF16)
    offset = offset_v[...].astype(F32).astype(BF16)
    lane = iota((LINKS, 128), 1)
    column = iota((LINKS, 128), 0)
    low = jnp.where((lax.rem(lane, LINKS) == column) & (lane < 64), 1.0, 0.0).astype(BF16)
    rows = dot(tree, low) * 32.0 + dot(offset, low)
    own_row = lane // LINKS == column
    table_row = jnp.sum(jnp.where(own_row, rows, 0.0), axis=0, keepdims=True)
    table_row = table_row.astype(jnp.int32)
    table_send[...] = table_row

    get_x.wait()
    get_basis.wait()
    coefs = [
        dot_nt(x_v[:, l * WIDTH : (l + 1) * WIDTH], basis_v[l]).astype(BF16) for l in range(LEAVES)
    ]
    for l in range(0, LEAVES, 2):
        coef_send[l // 2] = jnp.concatenate(
            [coefs[l].astype(F32), coefs[l + 1].astype(F32)], axis=1
        ).astype(BF16)
    get_trans.wait()
    terms = [dot(coefs[l], trans_v[l]) for l in range(LEAVES)]
    partial = functools.reduce(jnp.add, terms)
    part_send[...] = jnp.concatenate([partial[0 : NVEC // 2], partial[NVEC // 2 :]], axis=1)

    def send_part(leaf, s):
        send(part_send, part_recv.at[late, sub], part_ssem, part_rsem.at[late], leaf, s)

    def send_coefs(leaf, s):
        send(coef_send, coef_recv.at[late * SUBS + sub], coef_ssem, coef_rsem.at[late], leaf, s)

    @pl.when(late == 0)
    def _():
        pl.semaphore_wait(barrier, HOMES - 1 + SUBS - 1 + 2)
        for i in range(1, SUBS):
            send_part(me, lax.rem(sub + i, SUBS))
        for i in range(1, SUBS):
            send_coefs(me, lax.rem(sub + i, SUBS))
        coef_recv[pl.ds(sub, 1)] = coef_send[...][None]
        part_recv[0, pl.ds(sub, 1)] = part_send[...][None]

    @pl.when(late == 1)
    def _():
        pl.semaphore_wait(barrier, HOMES + 7 + 3 + 2 * (SUBS - 1) + 2)
        for i in range(SUBS):
            send_part(other, lax.rem(sub + i, SUBS))
        for i in range(SUBS):
            send_coefs(other, lax.rem(sub + i, SUBS))
        for i in range(1, SUBS):
            send(
                coef_send, coef_recv.at[SUBS + sub], coef_ssem, coef_rsem.at[1],
                me, lax.rem(sub + i, SUBS),
            )
        coef_recv[pl.ds(SUBS + sub, 1)] = coef_send[...][None]

    @pl.when(late == 0)
    def _():
        table_recv[pl.ds(j, 1)] = table_send[...][None]

        def ask(i, carry):
            leaf = home_leaf(lax.rem(j + i, HOMES))
            send(table_send, table_recv.at[j], table_ssem, table_rsem.at[0], leaf, sub)
            return carry

        lax.fori_loop(1, HOMES, ask, 0, unroll=True)

    @pl.when(late == 1)
    def _():
        def ask(i, carry):
            leaf = home_leaf(lax.rem(j + i, HOMES))
            send(table_send, table_recv.at[HOMES + j], table_ssem, table_rsem.at[1], leaf, sub)
            return carry

        send(top_slot_v, client_v, client_sem.at[0], client_sem.at[1], other, sub)
        for i in range(1, 8):
            leaf = mirror(home_leaf(row + lax.rem(j + i, 8)))
            send(table_send, table_recv.at[HOMES + j], table_ssem, table_rsem.at[1], leaf, sub)
        lax.fori_loop(0, HOMES, ask, 0)
        table_recv[pl.ds(HOMES + j, 1)] = table_send[...][None]

    for side, by, start in ((0, 1, (LEAVES - 1) * WIDTH), (1, -1, 0)):
        leaf, s = step(me, sub, by)
        leaf, kind = home_of(leaf)
        send(
            vec_hbm.at[:, pl.ds(start, WIDTH)], halo_v.at[kind, side],
            halo_ssem, halo_rsem.at[kind, side], leaf, s,
        )

    entry = iota((64, LINKS), 0)
    link = iota((64, LINKS), 1)
    pick_row = jnp.where(entry // LINKS == link, 1.0, 0.0).astype(BF16)
    by_entry = dot(pick_row, tree)
    tree_col = jnp.sum(
        jnp.where(lax.rem(entry, LINKS) == link, by_entry, 0.0), axis=1, keepdims=True
    )
    tree_row = (table_row[:, 0:64] >> 5).astype(F32)
    same = (tree_col == tree_row) & (iota((64, 64), 1) < iota((64, 64), 0))
    rank_col = jnp.sum(jnp.where(same, 1.0, 0.0), axis=1, keepdims=True)
    rank_v[...] = jnp.broadcast_to(rank_col, (64, 128))

    get_far.wait()
    for l in range(LEAVES):
        for f in range(0, LINKS, 2):
            pairs_v[l, :, f * RANK : (f + 2) * RANK] = jnp.concatenate(
                [far_v[l, f], far_v[l, f + 1]], axis=1
            )

    get_root.wait()
    for f in range(0, LINKS, 2):
        root_pairs_v[:, f * RANK : (f + 2) * RANK] = jnp.concatenate(
            [root_v[0, f], root_v[0, f + 1]], axis=1
        )

    def near(l, before, after):
        middle = x_v[:, l * WIDTH : (l + 1) * WIDTH]
        span = jnp.concatenate([before, middle, after], axis=1)
        local_v[:, l * WIDTH : (l + 1) * WIDTH] = dot_nt(span, near_v[l])

    for l in range(1, LEAVES - 1):
        get_near[l].wait()
        near(l, x_v[:, (l - 1) * WIDTH : l * WIDTH], x_v[:, (l + 1) * WIDTH : (l + 2) * WIDTH])
    get_near[0].wait()
    get_near[LEAVES - 1].wait()
    get_slot.wait()
    get_top_slot.wait()

    @pl.when(late == 1)
    def _():
        drain(table_recv.at[pl.ds(0, 7)], table_rsem.at[1])
        rows = table_recv.at[pl.ds(HOMES + row, 8)]
        for i in range(1, 4):
            leaf = mirror(home_leaf(lax.rem(j + 8 * i, HOMES)))
            send(rows, rows, pass_sem.at[0], pass_sem.at[1], leaf, sub)

    earlier = jnp.where(iota((64, 64), 0) < iota((64, 64), 1), 1.0, 0.0).astype(BF16)
    row_no = iota((HOMES, SUBS * LEAVES), 1) + 1

    def plan(kind, asker, tree_id):
        table = table_recv[asker * HOMES : (asker + 1) * HOMES, 0, :][:, 0:64]
        asked = (table >> 5) == tree_id
        pair = (table & 31) >> 1
        odd = table & 1
        order = dot(jnp.where(asked, 1.0, 0.0).astype(BF16), earlier)
        rows = (
            jnp.where(asked & (order == 0.0), (pair + 16 * odd + 1).astype(F32), 0.0),
            jnp.where(asked & (order == 1.0), (pair + 16 - 16 * odd + 1).astype(F32), 0.0),
        )
        plan_v[2 * asker + kind] = jnp.concatenate(
            [
                jnp.where(
                    jnp.sum(r, axis=1, keepdims=True).astype(jnp.int32) == row_no, 1.0, 0.0
                )
                for r in rows
            ],
            axis=0,
        ).astype(BF16)

    def fill(kind, asker):
        at = 2 * asker + kind
        left = iota((HOMES, 128), 1) < 64
        onehot = plan_v[at]
        boths = [dot(onehot, both_v[kind, v]) for v in range(NVEC)]
        for v in range(NVEC):
            picked_v[at, :, v, :] = jnp.where(left, boths[v][0:HOMES], boths[v][HOMES:])
        reply_send[at * HOMES : (at + 1) * HOMES] = picked_v[at].astype(BF16)

    def sums(kind):
        node = functools.reduce(jnp.add, [part_recv[kind, i] for i in range(SUBS)]).astype(BF16)
        node_send[kind] = node
        node_recv[pl.ds(kind * HOMES + j, 1)] = node[None]

    def unpack(kind):
        pairs = coef_recv[kind * SUBS : (kind + 1) * SUBS]
        wide_v[kind] = pairs.reshape(SUBS * LEAVES // 2, NVEC, 128).astype(F32)
        for v in range(NVEC):
            straight = wide_v[kind, :, v, :]
            turned = pltpu.roll(straight, 64, 1)
            both_v[kind, v] = jnp.concatenate([straight, turned], axis=0).astype(BF16)

    def spread_nodes(kind):
        def one(i, carry):
            leaf = home_leaf(lax.rem(j + i, HOMES))
            send(node_send.at[kind], node_recv.at[kind * HOMES + j], node_ssem, node_rsem, leaf, sub)
            return carry

        lax.fori_loop(1, HOMES, one, 0, unroll=True)

    def reply(kind, asker):
        def one(i, carry):
            to = lax.rem(j + i, HOMES)
            leaf = home_leaf(to)
            if asker:
                leaf = mirror(leaf)
            send(
                reply_send.at[(2 * asker + kind) * HOMES + to], reply_recv.at[kind * HOMES + j],
                reply_ssem, reply_rsem, leaf, sub,
            )
            return carry

        lax.fori_loop(0 if kind < asker else 1, HOMES, one, 0, unroll=True)
        if kind >= asker:
            reply_recv[pl.ds(kind * HOMES + j, 1)] = reply_send[
                pl.ds((2 * asker + kind) * HOMES + j, 1)
            ]

    def near_ends():
        zero = jnp.zeros((NVEC, WIDTH), BF16)
        first = (me == 0) & (sub == 0)
        last = (me == TREES - 1) & (sub == SUBS - 1)
        near(0, jnp.where(first, zero, halo_v[0, 0]), x_v[:, WIDTH : 2 * WIDTH])
        near(
            LEAVES - 1,
            x_v[:, (LEAVES - 2) * WIDTH : (LEAVES - 1) * WIDTH],
            jnp.where(last, zero, halo_v[0, 1]),
        )

    @pl.when(late == 0)
    def _():
        drain(part_recv.at[0, pl.ds(0, SUBS - 1)], part_rsem.at[0])
        sums(0)
        spread_nodes(0)
        drain(coef_recv.at[pl.ds(0, SUBS - 1)], coef_rsem.at[0])
        unpack(0)
        drain(table_recv.at[pl.ds(0, HOMES - 1)], table_rsem.at[0])
        plan(0, 0, me)
        plan(1, 0, other)
        fill(0, 0)
        reply(0, 0)
        drain(part_recv.at[1], part_rsem.at[1])
        sums(1)
        spread_nodes(1)
        drain(coef_recv.at[pl.ds(SUBS, SUBS)], coef_rsem.at[1])
        unpack(1)
        fill(1, 0)
        reply(1, 0)
        drain(table_recv.at[pl.ds(0, HOMES)], table_rsem.at[1])
        drain(client_v, client_sem.at[1])
        get_client = pltpu.make_async_copy(client_v, client_s, sem_smem.at[0])
        get_client.start()
        get_client.wait()
        plan(0, 1, me)
        fill(0, 1)
        reply(0, 1)
        for kind in range(2):
            for side in range(2):
                drain(halo_v.at[kind, side], halo_rsem.at[kind, side])
        send(halo_v.at[1], halo_v.at[0], fwd_sem.at[0], fwd_sem.at[1], other, sub)
        near_ends()
        drain(node_recv.at[pl.ds(0, 2 * HOMES - 2)], node_rsem)
        for f in range(LINKS):
            node_mine[f] = node_recv[top_slot_s[0, f]]

    @pl.when(late == 1)
    def _():
        drain(coef_recv.at[pl.ds(0, SUBS - 1)], coef_rsem.at[1])
        unpack(1)
        drain(table_recv.at[pl.ds(0, 24)], pass_sem.at[1])
        plan(1, 1, me)
        fill(1, 1)
        reply(1, 1)
        drain(halo_v.at[0], fwd_sem.at[1])
        near_ends()
        drain(node_mine, pick_sem.at[1])

    left = iota((NVEC // 2, 128), 1) < 64
    parts = []
    for f in range(0, LINKS, 2):
        even, odd = node_mine[f].astype(F32), node_mine[f + 1].astype(F32)
        top = jnp.where(left, even, pltpu.roll(odd, 64, 1))
        bottom = jnp.where(left, pltpu.roll(even, 64, 1), odd)
        parts.append(jnp.concatenate([top, bottom], axis=0))
    root_local = dot_nt(jnp.concatenate(parts, axis=1).astype(BF16), root_pairs_v[...])
    hi = root_local.astype(BF16)
    rest = root_local - hi.astype(F32)
    mid = rest.astype(BF16)
    lo = (rest - mid.astype(F32)).astype(BF16)
    three = jnp.concatenate([hi, mid, lo], axis=0)
    terms = [dot_nt(three, trans_v[l]) for l in range(LEAVES)]
    for l in range(LEAVES):
        t = terms[l]
        down_v[l] = t[0:NVEC] + t[NVEC : 2 * NVEC] + t[2 * NVEC : 3 * NVEC]

    @pl.when(late == 0)
    def _():
        for f in range(LINKS):
            node_theirs[f] = node_recv[client_s[0, f]]
        send(node_theirs, node_mine, pick_sem.at[0], pick_sem.at[1], other, sub)
        drain(reply_recv.at[pl.ds(0, 2 * HOMES - 2)], reply_rsem)

    @pl.when(late == 1)
    def _():
        drain(reply_recv.at[pl.ds(0, 2 * HOMES - 1)], reply_rsem)

    left = iota((NVEC, 128), 1) < 64
    coefs = []
    for l in range(LEAVES):
        parts = []
        for f in range(0, LINKS, 2):
            halves = []
            for k in range(2):
                e = l * LINKS + f + k
                got = reply_recv[slot_s[l, f + k]].astype(F32)
                there = jnp.broadcast_to(rank_v[e : e + 1, :], (NVEC, 128)) == float(k)
                halves.append(jnp.where(there, got, pltpu.roll(got, 64, 1)))
            parts.append(jnp.where(left, halves[0], halves[1]))
        coefs.append(jnp.concatenate(parts, axis=1).astype(BF16))
    fars = [dot_nt(coefs[l], pairs_v[l]) for l in range(LEAVES)]
    downs = [(fars[l] + down_v[l]).astype(BF16) for l in range(LEAVES)]
    outs = [dot(downs[l], basis_v[l]) for l in range(LEAVES)]
    for l in range(LEAVES):
        here = slice(l * WIDTH, (l + 1) * WIDTH)
        out_ref[:, here] = (local_v[:, here] + outs[l]).astype(BF16)

    drain(halo_v.at[0], halo_ssem)

    @pl.when(late == 0)
    def _():
        drain(coef_recv.at[pl.ds(0, SUBS - 1)], coef_ssem)
        drain(part_recv.at[0, pl.ds(0, SUBS - 1)], part_ssem)
        drain(table_recv.at[pl.ds(0, HOMES - 1)], table_ssem)
        drain(node_recv.at[pl.ds(0, 2 * HOMES - 2)], node_ssem)
        drain(reply_send.at[pl.ds(0, 3 * HOMES - 2)], reply_ssem)
        drain(halo_v.at[1], fwd_sem.at[0])
        drain(node_theirs, pick_sem.at[0])

    @pl.when(late == 1)
    def _():
        drain(coef_recv.at[pl.ds(0, 2 * SUBS - 1)], coef_ssem)
        drain(part_recv.at[0], part_ssem)
        drain(table_recv.at[pl.ds(0, HOMES + 7)], table_ssem)
        drain(table_recv.at[pl.ds(0, 24)], pass_sem.at[0])
        drain(client_v, client_sem.at[0])
        drain(reply_send.at[pl.ds(0, HOMES - 1)], reply_ssem)


def shards(vectors, basis, near, transfer, tree, offset, far, top, root):
    dma = pltpu.SemaphoreType.DMA
    i32 = jnp.int32
    scratch = [
        pltpu.VMEM((NVEC, LEAVES * WIDTH), BF16),
        pltpu.VMEM((LEAVES, RANK, WIDTH), BF16),
        pltpu.VMEM((LEAVES, WIDTH, 3 * WIDTH), BF16),
        pltpu.VMEM((LEAVES, RANK, RANK), BF16),
        pltpu.VMEM((LEAVES, LINKS), i32),
        pltpu.VMEM((LEAVES, LINKS), i32),
        pltpu.VMEM((LEAVES, LINKS, RANK, RANK), BF16),
        pltpu.VMEM((1, LINKS, RANK, RANK), BF16),
        pltpu.VMEM((1, LINKS), i32),
        pltpu.VMEM((LEAVES, LINKS), i32),
        pltpu.VMEM((1, LINKS), i32),
        pltpu.VMEM((1, LINKS), i32),
        pltpu.SMEM((LEAVES, LINKS), i32),
        pltpu.SMEM((1, LINKS), i32),
        pltpu.SMEM((1, LINKS), i32),
        pltpu.VMEM((1, 128), i32),
        pltpu.VMEM((2 * HOMES, 1, 128), i32),
        pltpu.VMEM((LEAVES // 2, NVEC, 128), BF16),
        pltpu.VMEM((2 * SUBS, LEAVES // 2, NVEC, 128), BF16),
        pltpu.VMEM((NVEC // 2, 128), F32),
        pltpu.VMEM((2, SUBS, NVEC // 2, 128), F32),
        pltpu.VMEM((2, SUBS * LEAVES // 2, NVEC, 128), F32),
        pltpu.VMEM((2, NVEC, SUBS * LEAVES, 128), BF16),
        pltpu.VMEM((4, 2 * HOMES, SUBS * LEAVES), BF16),
        pltpu.VMEM((2, NVEC // 2, 128), BF16),
        pltpu.VMEM((2 * HOMES, NVEC // 2, 128), BF16),
        pltpu.VMEM((LINKS, NVEC // 2, 128), BF16),
        pltpu.VMEM((LINKS, NVEC // 2, 128), BF16),
        pltpu.VMEM((2, 2, NVEC, WIDTH), BF16),
        pltpu.VMEM((4 * HOMES, NVEC, 128), BF16),
        pltpu.VMEM((2 * HOMES, NVEC, 128), BF16),
        pltpu.VMEM((4, HOMES, NVEC, 128), F32),
        pltpu.VMEM((64, 128), F32),
        pltpu.VMEM((LEAVES, RANK, LINKS * RANK), BF16),
        pltpu.VMEM((RANK, LINKS * RANK), BF16),
        pltpu.VMEM((LEAVES, NVEC, RANK), F32),
        pltpu.VMEM((NVEC, LEAVES * WIDTH), F32),
        dma,
        dma,
        dma((LEAVES,)),
        dma,
        dma((3,)),
        dma,
        dma,
        dma((2,)),
        dma,
        dma((2, 2)),
        dma,
        dma((2,)),
        dma,
        dma((2,)),
        dma,
        dma((2,)),
        dma,
        dma,
        dma,
        dma,
        dma((2,)),
        dma((2,)),
        dma((2,)),
        dma((2,)),
    ]
    return pl.pallas_call(
        kernel,
        out_shape=jax.ShapeDtypeStruct(vectors.shape, BF16),
        in_specs=[pl.BlockSpec(memory_space=pl.ANY)] * 9,
        out_specs=pl.BlockSpec(memory_space=pltpu.VMEM),
        scratch_shapes=scratch,
        compiler_params=pltpu.CompilerParams(
            collective_id=0, has_side_effects=True, vmem_limit_bytes=40 * 2**20
        ),
        name="product",
    )(*[
        pltpu.with_memory_space_constraint(a, pltpu.HBM)
        for a in (vectors, basis, near, transfer, tree, offset, far, top, root)
    ])


def solution(mesh):
    placed = (
        P(None, ("leaf", "sub")),
        P(("leaf", "sub"), None, None),
        P(("leaf", "sub"), None, None),
        P(("leaf", "sub"), None, None),
        P(("leaf", "sub"), None),
        P(("leaf", "sub"), None),
        P(("leaf", "sub"), None, None, None),
        P("leaf", None),
        P("leaf", None, None, None),
    )
    return jax.shard_map(
        shards, mesh=mesh, in_specs=placed, out_specs=P(None, ("leaf", "sub")), check_vma=False
    )
```
